256 devices in a mesh: tok: 16 (over z, core), rep: 16 (over x, y).
Axes of the slice: x: 4, y: 4, z: 8, core: 2. Of those that a mesh axis runs over, the one named last changes fastest.
Arguments:
- hidden_in: bfloat16 [8192, 4096], P('tok', 'rep'), may hold values from -9 to 9
- w_query: bfloat16 [4096, 4096], P(None, 'rep'), may hold values from -2 to 2
- w_key: bfloat16 [4096, 4096], P(None, 'rep'), may hold values from -2 to 2
- w_value: bfloat16 [4096, 4096], P(None, 'rep'), may hold values from -0.09375 to 0.09375
- w_out: bfloat16 [4096, 4096], P('rep'), may hold values from -3 to 3
- q_gain: float32 [4096], P('rep'), may hold values from 0.5 to 6
- k_gain: float32 [4096], P('rep'), may hold values from 0.5 to 6
- post_gain: float32 [4096], P('rep'), may hold values from 0.1 to 1.9
- prompt_lengths: int32 [8], replicated, may hold values from 1 to 4096, as said below
- segment_ids: int32 [8192], replicated, may hold values from 0 to 7, as said below
- deal: int32 [8192], replicated, may hold values from 0 to 8191, as said below
- inverse: int32 [8192], replicated, may hold values from 0 to 8191, as said below
- slots: int32 [8192], replicated, may hold values from 0 to 8191, as said below
Outputs:
- output: bfloat16 [8192, 4096], P('tok', 'rep')
- cache_keys: bfloat16 [8192, 4096], P('tok', 'rep')
- cache_values: bfloat16 [8192, 4096], P('tok', 'rep')
The draws below stay inside these ranges and needn't reach their ends.
Inputs may be any that keep to these rules, and one draw needn't show every extreme that they name: `prompt_lengths`: the lengths sum to 8192; the longest prompt has exactly 4096 tokens. `segment_ids`: prompts lie in order: prompt s holds the prompt_lengths[s] packed tokens after those of prompts 0 to s - 1. `deal`: A permutation. For any two indices a and b of tok, exactly 32 of the packed tokens a * 512 to (a + 1) * 512 - 1 sit in dealt rows b * 512 to (b + 1) * 512 - 1. inverse[deal[q]] = q for every dealt row q. `slots`: A permutation. For any two indices a and b of tok, exactly 32 of the dealt rows a * 512 to (a + 1) * 512 - 1 have cache rows b * 512 to (b + 1) * 512 - 1.
All inputs are finite; a program needn't handle non-finite values.
Results may differ from the reference program's by a relative error of at most 0.012.
Values may be sent and summed in bfloat16 or wider, within the bound.
No kernel may reach another device: no remote copies, remote signals or barrier semaphores. Data moves between devices by JAX's collectives and lax.ppermute only.
A program may use at most 128 MiB of HBM per device.

```python
import math
import jax
import jax.numpy as jnp
from jax import lax

D = 4096
HEADS = 32
HEAD_DIM = 128
TOK_DEV = 512
NSEG = 8
TOKENS = 8192
MAXLEN = 4096


def bounded(key, shape):
    return jax.random.truncated_normal(key, -3.0, 3.0, shape, jnp.float32)


def projection_pair(key):
    lower_draw = bounded(jax.random.fold_in(key, 11), (D, D))
    upper_draw = bounded(jax.random.fold_in(key, 12), (D, D))
    wobble = jnp.exp(jax.random.uniform(jax.random.fold_in(key, 13), (1, D), jnp.float32, -0.7, 0.7))
    head_index = jnp.arange(HEADS, dtype=jnp.float32)
    head_scale = 0.6 * 3.0 ** (head_index / max(HEADS - 1, 1))
    scale = jnp.repeat(head_scale, HEAD_DIM)[None, :] * wobble / math.sqrt(D)
    key_part = upper_draw
    return (lower_draw * scale, key_part * scale)


def draw_w_query(key, part):
    return projection_pair(key)[0].astype(jnp.bfloat16)


def draw_w_key(key, part):
    return projection_pair(key)[1].astype(jnp.bfloat16)


def draw_w_out(key, part):
    base = bounded(jax.random.fold_in(key, 41), (D, D))
    columns = jnp.arange(D, dtype=jnp.float32)[None, :]
    scale = 0.6 * 3.0 ** (columns / max(D - 1, 1)) * jnp.exp(jax.random.uniform(jax.random.fold_in(key, 43), (1, D), jnp.float32, -0.7, 0.7))
    values = base * scale
    return (values / math.sqrt(D)).astype(jnp.bfloat16)


def draw_hidden_in(key, part):
    noise = bounded(jax.random.fold_in(key, 51), (TOKENS, D))
    row_scale = jnp.exp(jax.random.uniform(jax.random.fold_in(key, 53), (TOKENS, 1), jnp.float32, -0.7, 0.7))
    values = noise * row_scale
    return values.astype(jnp.bfloat16)


def gain_draw(key, salt):
    low_end, high_end = (0.5, 2.0)
    logs = jax.random.uniform(jax.random.fold_in(key, salt), (D,), jnp.float32, math.log(low_end), math.log(high_end))
    return jnp.exp(logs)


def draw_q_gain(key, part):
    return gain_draw(key, 61)


def draw_k_gain(key, part):
    return gain_draw(key, 62)


def pack_layout(key):
    remainder = TOKENS - MAXLEN
    picks = jax.random.permutation(jax.random.fold_in(key, 21), remainder - 1)[:NSEG - 2] + 1
    cuts = jnp.sort(picks.astype(jnp.int32))
    edges = jnp.concatenate([jnp.zeros((1,), jnp.int32), cuts, jnp.full((1,), remainder, jnp.int32)])
    pieces = edges[1:] - edges[:-1]
    lengths = jnp.concatenate([jnp.full((1,), MAXLEN, jnp.int32), pieces])
    offset = jax.random.randint(jax.random.fold_in(key, 22), (), 0, NSEG)
    lengths = jnp.roll(lengths, offset)
    prompt_ends = jnp.cumsum(lengths)
    token_ids = jnp.arange(TOKENS, dtype=jnp.int32)
    segments = jnp.sum((token_ids[:, None] >= prompt_ends[None, :]).astype(jnp.int32), axis=1)
    return (lengths, segments)


def draw_prompt_lengths(key, part):
    return pack_layout(key)[0]


def draw_segment_ids(key, part):
    return pack_layout(key)[1]


def deal_layout(key):
    shards = TOKENS // TOK_DEV
    group_size = TOK_DEV // shards

    def ranking(salt):
        split_keys = jax.random.split(jax.random.fold_in(key, salt), shards)
        return jax.vmap(lambda single: jax.random.permutation(single, TOK_DEV))(split_keys).astype(jnp.int32)

    def spread(ranks, within_order):
        target = ranks // group_size
        within = ranks % group_size
        source = jnp.arange(shards, dtype=jnp.int32)[:, None]
        placed = within_order[target, source * group_size + within]
        return (target * TOK_DEV + placed).reshape(-1).astype(jnp.int32)
    inverse_rows = spread(ranking(31), ranking(32))
    deal_rows = jnp.argsort(inverse_rows).astype(jnp.int32)
    slot_rows = spread(ranking(33), ranking(34))
    return (deal_rows, inverse_rows, slot_rows)


def draw_deal(key, part):
    return deal_layout(key)[0]


def draw_inverse(key, part):
    return deal_layout(key)[1]


def draw_slots(key, part):
    return deal_layout(key)[2]


def shard_levels(key, dims, cuts, low, largest):
    level, own = 1.0, jax.random.fold_in(key, 6)
    for axis_at, parts in cuts:
        draws = jnp.exp(jax.random.uniform(jax.random.fold_in(own, axis_at), (parts,), jnp.float32, low / len(cuts), largest / len(cuts)))
        level = level * jnp.repeat(draws, dims[axis_at] // parts).reshape([-1 if axis == axis_at else 1 for axis in range(len(dims))])
    return level


def gaussian(rng, extent, deviation, most, cuts=(), kind=jnp.bfloat16):
    values = jax.random.normal(rng, extent, jnp.float32) * deviation
    if len(cuts) > 0:
        values = shard_levels(rng, extent, cuts, -0.22, 0.18) * values
    return jnp.clip(values, min=-most, max=most).astype(kind)


def setup_inputs(seed: int = 0) -> dict:
    key_list = jax.random.split(jax.random.key(seed), 14)
    return {
        "hidden_in": draw_hidden_in(jax.random.fold_in(key_list[13], 71), 0),
        "w_query": draw_w_query(jax.random.fold_in(key_list[13], 71), 0),
        "w_key": draw_w_key(jax.random.fold_in(key_list[13], 71), 0),
        "w_value": gaussian(key_list[3], (D, D), D ** -0.5, 0.09375, ((1, 16),)),
        "w_out": draw_w_out(jax.random.fold_in(key_list[13], 71), 0),
        "q_gain": draw_q_gain(jax.random.fold_in(key_list[13], 71), 0),
        "k_gain": draw_k_gain(jax.random.fold_in(key_list[13], 71), 0),
        "post_gain": jnp.clip(1.0 + 0.18 * jax.random.normal(key_list[7], (D,), jnp.float32), 0.1, 1.9),
        "prompt_lengths": draw_prompt_lengths(jax.random.fold_in(key_list[13], 71), 0),
        "segment_ids": draw_segment_ids(jax.random.fold_in(key_list[13], 71), 0),
        "deal": draw_deal(jax.random.fold_in(key_list[13], 71), 0),
        "inverse": draw_inverse(jax.random.fold_in(key_list[13], 71), 0),
        "slots": draw_slots(jax.random.fold_in(key_list[13], 71), 0),
    }


EPSILON = 1e-06
ROPE_BASE = 500000.0

def rotate(values, positions):
    half_size = values.shape[-1] // 2
    frequency = ROPE_BASE ** (-jnp.arange(half_size, dtype=jnp.float32) * 2.0 / values.shape[-1])
    angles = positions.astype(jnp.float32)[:, None] * frequency[None, :]
    cosine = jnp.cos(angles)[:, None, :]
    sine_part = jnp.sin(angles)[:, None, :]
    lower_half = values[..., :half_size]
    upper_half = values[..., half_size:]
    return jnp.concatenate([lower_half * cosine - upper_half * sine_part, upper_half * cosine + lower_half * sine_part], axis=-1)

def reference(hidden_in, w_query, w_key, w_value, w_out, q_gain, k_gain, post_gain, prompt_lengths, segment_ids, deal, inverse, slots):
    packed = hidden_in[inverse]
    query_rows = jnp.dot(packed, w_query, preferred_element_type=jnp.float32)
    key_rows = jnp.dot(packed, w_key, preferred_element_type=jnp.float32)
    value_half = jnp.dot(packed, w_value, preferred_element_type=jnp.float32).astype(jnp.bfloat16)
    prompt_starts = jnp.cumsum(prompt_lengths) - prompt_lengths
    token_ids = jnp.arange(TOKENS, dtype=jnp.int32)
    positions = token_ids - prompt_starts[segment_ids]
    query_rows = query_rows * lax.rsqrt(lax.optimization_barrier(jnp.mean(query_rows * query_rows, axis=1, keepdims=True)) + EPSILON) * q_gain[None, :]
    key_rows = key_rows * lax.rsqrt(lax.optimization_barrier(jnp.mean(key_rows * key_rows, axis=1, keepdims=True)) + EPSILON) * k_gain[None, :]
    query_rot = rotate(query_rows.reshape(TOKENS, HEADS, HEAD_DIM), positions).astype(jnp.bfloat16)
    key_rot = rotate(key_rows.reshape(TOKENS, HEADS, HEAD_DIM), positions).astype(jnp.bfloat16)
    allowed = (segment_ids[:, None] == segment_ids[None, :]) & (token_ids[None, :] <= token_ids[:, None])
    scale = HEAD_DIM ** (-0.5)

    def one_head(operands):
        head_query, head_key, head_value = operands
        scores = jnp.dot(head_query.astype(jnp.float32), head_key.astype(jnp.float32).T) * scale
        masked = jnp.where(allowed, scores, -1e+30)
        row_top = lax.optimization_barrier(jnp.max(masked, axis=1, keepdims=True))
        weights = jnp.where(allowed, jnp.exp(masked - row_top), 0.0)
        totals = lax.optimization_barrier(jnp.sum(weights, axis=1, keepdims=True))
        rounded = lax.optimization_barrier(weights.astype(jnp.bfloat16))
        return jnp.dot(rounded.astype(jnp.float32), head_value.astype(jnp.float32)) / totals
    value_heads = value_half.reshape(TOKENS, HEADS, HEAD_DIM)
    per_head = lax.map(one_head, (query_rot.transpose(1, 0, 2), key_rot.transpose(1, 0, 2), value_heads.transpose(1, 0, 2)))
    attended = per_head.transpose(1, 0, 2).reshape(TOKENS, D).astype(jnp.bfloat16)
    mixed = jnp.dot(attended, w_out, preferred_element_type=jnp.float32)
    normed = mixed * lax.rsqrt(lax.optimization_barrier(jnp.mean(mixed * mixed, axis=1, keepdims=True)) + EPSILON) * post_gain[None, :]
    output = (packed.astype(jnp.float32) + normed).astype(jnp.bfloat16)
    key_flat = key_rot.reshape(TOKENS, D)
    cache_keys = jnp.zeros((TOKENS, D), jnp.bfloat16).at[slots].set(key_flat[deal])
    cache_values = jnp.zeros((TOKENS, D), jnp.bfloat16).at[slots].set(value_half[deal])
    return (output, cache_keys, cache_values)
```

```python
import functools
import math

import jax
import jax.numpy as jnp
from jax import lax
from jax.experimental import pallas as pl
from jax.experimental.pallas import tpu as pltpu
from jax.sharding import Mesh
from jax.sharding import PartitionSpec as P

HEAD_DIM = 128
EPSILON = 1e-06
ROPE_BASE = 500000.0
SIDE = 4
RING = 8
TOK = ("z", "core")
REP = ("x", "y")
LOWEST = -1e30
FLOOR = -1e20
VMEM = 48 * 2**20


def plane_pairs(first, shift):
    pairs = []
    for core in range(2):
        for x in range(SIDE):
            for y in range(SIDE):
                along_x = (core == 0) == first
                to_x = (x + shift) % SIDE if along_x else x
                to_y = y if along_x else (y + shift) % SIDE
                pairs.append((core * 16 + x * 4 + y, core * 16 + to_x * 4 + to_y))
    return pairs


def plane_send(value, first, shift):
    return lax.ppermute(value, ("core", "x", "y"), plane_pairs(first, shift))


def ring_send(value, shift):
    return lax.ppermute(value, "z", [(i, (i + shift) % RING) for i in range(RING)])


def core_swap(value):
    return lax.ppermute(value, "core", [(0, 1), (1, 0)])


def spread(value, axes, size):
    copies = jnp.broadcast_to(value[None], (size, *value.shape))
    return lax.all_to_all(copies, axes, 0, 0, tiled=True)


def block_ids(column, core, x, y):
    first = jnp.where(core == 0, x, y)
    second = (jnp.where(core == 0, y, x) + column) % SIDE
    steps = jnp.array([0, 3, 1, 2], jnp.int32)
    mine = (first + steps) % SIDE
    return jnp.where(core == 0, mine * SIDE + second, second * SIDE + mine).astype(jnp.int32)


def block_matmul(arrays, ids, weights, acc, finish=None, extras=(), outs=None, core=None):
    counts = [a.shape[0] for a in arrays]
    rows, depth = arrays[0].shape[1:]
    widths = [w.shape[1] for w in weights]
    total = sum(widths)
    steps = sum(counts)
    starts = [sum(counts[:i]) for i in range(len(counts))]
    n_arrays, n_weights, n_extras = len(arrays), len(weights), len(extras)
    has_acc = acc is not None
    if outs is None:
        outs = [jax.ShapeDtypeStruct((rows, total), jnp.float32)]
    n_outs = len(outs)

    def kernel(ids_ref, *refs):
        step = pl.program_id(0)
        array_refs, refs = refs[:n_arrays], refs[n_arrays:]
        weight_refs, refs = refs[:n_weights], refs[n_weights:]
        if has_acc:
            acc_ref, refs = refs[0], refs[1:]
        extra_refs, refs = refs[:n_extras], refs[n_extras:]
        out_refs, sum_ref = refs[:n_outs], refs[n_outs]

        @pl.when(step == 0)
        def _():
            sum_ref[...] = acc_ref[...] if has_acc else jnp.zeros_like(sum_ref)

        for ref, start, count in zip(array_refs, starts, counts):

            @pl.when((step >= start) & (step < start + count))
            def _():
                at = 0
                for w_ref, width in zip(weight_refs, widths):
                    sum_ref[:, at : at + width] += jnp.dot(
                        ref[0], w_ref[...], preferred_element_type=jnp.float32
                    )
                    at += width

        @pl.when(step == steps - 1)
        def _():
            if finish is None:
                out_refs[0][...] = sum_ref[...]
            else:
                finish(ids_ref[steps], sum_ref, extra_refs, out_refs)

    def pick(start, count):
        return lambda i, ids_ref: (jnp.clip(i - start, 0, count - 1), 0, 0)

    def whole(shape):
        return pl.BlockSpec(shape, lambda i, ids_ref: (0,) * len(shape))

    in_specs = [pl.BlockSpec((1, rows, depth), pick(s, n)) for s, n in zip(starts, counts)]
    in_specs += [pl.BlockSpec((depth, w), lambda i, ids_ref: (ids_ref[i], 0)) for w in widths]
    operands = [*arrays, *weights]
    if has_acc:
        in_specs.append(whole(acc.shape))
        operands.append(acc)
    in_specs += [whole(e.shape) for e in extras]
    operands += list(extras)
    tail = jnp.zeros((1,), jnp.int32) if core is None else core.reshape(1).astype(jnp.int32)
    return pl.pallas_call(
        kernel,
        grid_spec=pltpu.PrefetchScalarGridSpec(
            num_scalar_prefetch=1,
            grid=(steps,),
            in_specs=in_specs,
            out_specs=[whole(o.shape) for o in outs],
            scratch_shapes=[pltpu.VMEM((rows, total), jnp.float32)],
        ),
        out_shape=outs,
        compiler_params=pltpu.CompilerParams(vmem_limit_bytes=VMEM),
        cost_estimate=pl.CostEstimate(
            flops=2 * rows * depth * total * steps,
            bytes_accessed=steps * depth * (rows + total) * 2 + rows * total * 8,
            transcendentals=0,
        ),
    )(jnp.concatenate([ids, tail]), *operands)


def gathered_matmul(block, weights, core, x, y, finish, extras, outs):
    half = block.shape[0] // 2
    left = plane_send(block, True, 1)
    right = plane_send(block, True, -1)
    far_low = plane_send(left[:half], True, 1)
    far_high = plane_send(right[half:], True, -1)
    stack = jnp.stack([block, left, right, jnp.concatenate([far_low, far_high])])
    stack_left = plane_send(stack, False, 1)
    stack_right = plane_send(stack, False, -1)
    far_left = plane_send(stack_left[:2], False, 1)
    far_right = plane_send(stack_right[2:], False, -1)
    acc = block_matmul([stack], block_ids(0, core, x, y), weights, None)[0]
    near = jnp.concatenate([block_ids(3, core, x, y), block_ids(1, core, x, y)])
    acc = block_matmul([stack_left, stack_right], near, weights, acc)[0]
    return block_matmul(
        [far_left, far_right], block_ids(2, core, x, y), weights, acc, finish, extras, outs, core
    )


def finish_projection(core, sum_ref, extras, outs):
    cos_ref, sin_ref, q_gain_ref, k_gain_ref = extras
    q_ref, k_ref, v_ref, keep_ref, give_ref, sums_ref = outs
    width = q_ref.shape[1]
    query = sum_ref[:, :width]
    key = sum_ref[:, width : 2 * width]
    value = sum_ref[:, 2 * width :].astype(jnp.bfloat16)
    q_sums = jnp.sum(query * query, axis=1, keepdims=True)
    k_sums = jnp.sum(key * key, axis=1, keepdims=True)
    lane = lax.broadcasted_iota(jnp.int32, sums_ref.shape, 1)
    sums_ref[...] = jnp.where(lane == 0, q_sums, k_sums)
    cosine, sine = cos_ref[...], sin_ref[...]
    query = query * q_gain_ref[...]
    key = key * k_gain_ref[...]
    v_ref[...] = value
    for head in range(2):
        at = slice(head * HEAD_DIM, (head + 1) * HEAD_DIM)
        q_head, k_head = query[:, at], key[:, at]
        q_rot = q_head * cosine + pltpu.roll(q_head, HEAD_DIM // 2, 1) * sine
        k_rot = k_head * cosine + pltpu.roll(k_head, HEAD_DIM // 2, 1) * sine
        k_half = k_rot.astype(jnp.bfloat16)
        q_ref[:, at] = q_rot.astype(jnp.bfloat16)
        k_ref[:, at] = k_half

        @pl.when(core == head)
        def _():
            keep_ref[:, :HEAD_DIM] = k_half
            keep_ref[:, HEAD_DIM:] = value[:, at]

        @pl.when(core != head)
        def _():
            give_ref[:, :HEAD_DIM] = k_half
            give_ref[:, HEAD_DIM:] = value[:, at]


def finish_output(core, sum_ref, extras, outs):
    mixed_ref, sums_ref = outs
    mixed = sum_ref[...]
    mixed_ref[...] = mixed
    sums_ref[...] = jnp.broadcast_to(
        jnp.sum(mixed * mixed, axis=1, keepdims=True), sums_ref.shape
    )


Q_TILE = 256
K_TILE = 512


def attend(query, q_scale, q_start, key_packed, key_scale, chunks, chips, place, state, last):
    rows = query.shape[0]
    n_chunks = len(chunks)
    has_state = state is not None

    def kernel(ids_ref, *refs):
        q_ref, scale_ref, start_ref, kp_ref, ks_ref, *refs = refs
        chunk_refs, refs = refs[:n_chunks], refs[n_chunks:]
        if has_state:
            top_in, total_in, sum_in, *refs = refs
        q_tile = q_ref[...]
        scale = scale_ref[...]
        start = start_ref[...]
        packed = (
            ids_ref[n_chunks] * rows
            + pl.program_id(0) * Q_TILE
            + lax.broadcasted_iota(jnp.int32, (Q_TILE, 1), 0)
        )
        if has_state:
            top, total, weighted = top_in[:, :1], total_in[:, :1], sum_in[...]
        else:
            top = jnp.full((Q_TILE, 1), FLOOR, jnp.float32)
            total = jnp.zeros((Q_TILE, 1), jnp.float32)
            weighted = jnp.zeros((Q_TILE, HEAD_DIM), jnp.float32)
        for i, (ref, (array, first)) in enumerate(zip(chunk_refs, chunks)):
            chip = ids_ref[i]
            for at in range(0, array.shape[0], K_TILE):
                keys = ref[at : at + K_TILE, :HEAD_DIM]
                values = ref[at : at + K_TILE, HEAD_DIM:]
                kp = kp_ref[chip, :, first + at : first + at + K_TILE]
                ks = ks_ref[chip, :, first + at : first + at + K_TILE]
                scores = lax.dot_general(
                    q_tile, keys, (((1,), (1,)), ((), ())), preferred_element_type=jnp.float32
                )
                allowed = (kp <= packed) & (kp >= start)
                scores = jnp.where(allowed, scores * scale * ks, LOWEST)
                new_top = jnp.maximum(top, jnp.max(scores, axis=1, keepdims=True))
                weights = jnp.exp2(scores - new_top)
                factor = jnp.exp2(top - new_top)
                total = total * factor + jnp.sum(weights, axis=1, keepdims=True)
                weighted = weighted * factor + jnp.dot(
                    weights.astype(jnp.bfloat16), values, preferred_element_type=jnp.float32
                )
                top = new_top
        if last:
            refs[0][0] = (weighted / total).astype(jnp.bfloat16)
        else:
            top_out, total_out, sum_out = refs
            top_out[...] = jnp.broadcast_to(top, top_out.shape)
            total_out[...] = jnp.broadcast_to(total, total_out.shape)
            sum_out[...] = weighted

    def tile(width):
        return pl.BlockSpec((Q_TILE, width), lambda i, ids_ref: (i, 0))

    def whole(shape):
        return pl.BlockSpec(shape, lambda i, ids_ref: (0,) * len(shape))

    in_specs = [tile(HEAD_DIM), tile(1), tile(1), whole(key_packed.shape), whole(key_scale.shape)]
    in_specs += [whole(a.shape) for a, _ in chunks]
    operands = [query, q_scale, q_start, key_packed, key_scale, *[a for a, _ in chunks]]
    if has_state:
        in_specs += [tile(HEAD_DIM)] * 3
        operands += list(state)
    if last:
        halves = rows // Q_TILE // 2
        out_shape = [jax.ShapeDtypeStruct((2, rows // 2, HEAD_DIM), jnp.bfloat16)]
        out_specs = [
            pl.BlockSpec(
                (1, Q_TILE, HEAD_DIM),
                lambda i, ids_ref: (
                    (i // halves + ids_ref[n_chunks + 1]) % 2,
                    i % halves,
                    0,
                ),
            )
        ]
    else:
        out_shape = [jax.ShapeDtypeStruct((rows, HEAD_DIM), jnp.float32)] * 3
        out_specs = [tile(HEAD_DIM)] * 3
    keys_seen = sum(a.shape[0] for a, _ in chunks)
    ids = jnp.concatenate([jnp.stack(chips), jnp.stack(place)]).astype(jnp.int32)
    return pl.pallas_call(
        kernel,
        grid_spec=pltpu.PrefetchScalarGridSpec(
            num_scalar_prefetch=1,
            grid=(rows // Q_TILE,),
            in_specs=in_specs,
            out_specs=out_specs,
        ),
        out_shape=out_shape,
        compiler_params=pltpu.CompilerParams(vmem_limit_bytes=VMEM),
        cost_estimate=pl.CostEstimate(
            flops=4 * rows * keys_seen * HEAD_DIM,
            bytes_accessed=rows * HEAD_DIM * 26 + keys_seen * 512,
            transcendentals=rows * keys_seen,
        ),
    )(ids, *operands)


def ranks_of(values):
    return jnp.sum((values[None, :] < values[:, None]).astype(jnp.int32), axis=1)


def within(sources):
    index = jnp.arange(sources.shape[0], dtype=jnp.int32)
    same = (sources[None, :] == sources[:, None]) & (index[None, :] < index[:, None])
    return jnp.sum(same.astype(jnp.int32), axis=1)


def place_rows(positions, rows):
    index = jnp.arange(rows.shape[0], dtype=jnp.int32)
    chosen = (positions[:, None] == index[None, :]).astype(jnp.bfloat16)
    return jnp.dot(chosen, rows, preferred_element_type=jnp.float32).astype(jnp.bfloat16)


def bucket_rows(ranks, rows):
    index = jnp.arange(rows.shape[0], dtype=jnp.int32)
    chosen = (ranks[None, :] == index[:, None]).astype(jnp.bfloat16)
    return jnp.dot(chosen, rows, preferred_element_type=jnp.float32).astype(jnp.bfloat16)


def body(
    hidden_in,
    w_query,
    w_key,
    w_value,
    w_out,
    q_gain,
    k_gain,
    post_gain,
    prompt_lengths,
    segment_ids,
    deal,
    inverse,
    slots,
):
    rows, width = hidden_in.shape
    full_width = w_query.shape[0]
    shards = 16
    share = rows // shards
    x, y = lax.axis_index("x"), lax.axis_index("y")
    z, core = lax.axis_index("z"), lax.axis_index("core")
    first_row = (z * 2 + core) * rows
    chip_row = z * 2 * rows

    prompt_ids = jnp.arange(prompt_lengths.shape[0], dtype=jnp.int32)
    prompt_starts = jnp.sum(
        jnp.where(prompt_ids[None, :] < prompt_ids[:, None], prompt_lengths[None, :], 0), axis=1
    )

    def start_of(packed):
        return jnp.max(
            jnp.where(prompt_starts[None, :] <= packed[:, None], prompt_starts[None, :], 0), axis=1
        )

    my_packed = lax.dynamic_slice_in_dim(deal, first_row, rows)
    positions = (my_packed - start_of(my_packed)).astype(jnp.float32)
    half = HEAD_DIM // 2
    frequency = ROPE_BASE ** (-jnp.arange(half, dtype=jnp.float32) * 2.0 / HEAD_DIM)
    angles = positions[:, None] * frequency[None, :]
    cosine, sine = jnp.cos(angles), jnp.sin(angles)
    cosine = jnp.concatenate([cosine, cosine], axis=1)
    sine = jnp.concatenate([-sine, sine], axis=1)

    half_rows = jax.ShapeDtypeStruct((rows, width), jnp.bfloat16)
    q_rot, k_rot, value, keep, give, sums = gathered_matmul(
        hidden_in,
        [w_query, w_key, w_value],
        core,
        x,
        y,
        finish_projection,
        [cosine, sine, q_gain[None, :], k_gain[None, :]],
        [half_rows] * 5 + [jax.ShapeDtypeStruct((rows, 128), jnp.float32)],
    )

    chunk = jnp.concatenate([keep, core_swap(give)])
    up, down = [chunk], [chunk]
    for _ in range(3):
        up.append(ring_send(up[-1], 1))
        down.append(ring_send(down[-1], -1))
    far_low = ring_send(up[3][:rows], 1)
    far_high = ring_send(down[3][rows:], -1)

    part_sums = sums[:, :2].T
    all_sums = jnp.sum(spread(part_sums, REP, 16), axis=0)
    scales = lax.rsqrt(all_sums / full_width + EPSILON)
    ranks = ranks_of(my_packed)
    index = jnp.arange(rows, dtype=jnp.int32)
    sorted_q_scale = jnp.sum(
        jnp.where(ranks[None, :] == index[:, None], scales[0][None, :], 0.0), axis=1
    )
    all_scales = spread(jnp.stack([sorted_q_scale, scales[1]]), TOK, shards)
    key_scale = all_scales[:, 1].reshape(RING, 2, rows)
    key_packed = deal.reshape(RING, 2, rows)
    key_scale = jnp.where(core == 0, key_scale, key_scale[:, ::-1]).reshape(RING, 1, 2 * rows)
    key_packed = jnp.where(core == 0, key_packed, key_packed[:, ::-1]).reshape(RING, 1, 2 * rows)

    bucketed = bucket_rows(ranks, jnp.concatenate([q_rot, hidden_in], axis=1))
    q_sent = bucketed[:, :width].reshape(RING, 2 * share, 2, HEAD_DIM)
    q_sent = q_sent.transpose(0, 2, 1, 3).reshape(shards, 2 * share, HEAD_DIM)
    h_sent = bucketed[:, width:].reshape(shards, share, 2, HEAD_DIM)
    h_sent = h_sent.transpose(0, 2, 1, 3).reshape(shards, 2 * share, HEAD_DIM)
    moved = lax.all_to_all(jnp.concatenate([q_sent, h_sent], axis=1), TOK, 0, 0, tiled=True)
    sources = lax.dynamic_slice_in_dim(inverse, chip_row, 2 * rows) // rows
    q_places = sources * (2 * share) + within(sources)
    my_sources = lax.dynamic_slice_in_dim(inverse, first_row, rows) // rows
    h_places = my_sources * share + within(my_sources)
    query = place_rows(q_places, moved[:, : 2 * share].reshape(2 * rows, HEAD_DIM))
    residual = moved[:, 2 * share :].reshape(shards, 2, share, HEAD_DIM)
    residual = place_rows(h_places, residual.transpose(0, 2, 1, 3).reshape(rows, width))
    arrived_scale = lax.dynamic_slice_in_dim(all_scales[:, 0], z * 2 * share, 2 * share, axis=1)
    arrived_scale = arrived_scale.reshape(2 * rows)
    index = jnp.arange(2 * rows, dtype=jnp.int32)
    q_scale = jnp.sum(
        jnp.where(q_places[:, None] == index[None, :], arrived_scale[None, :], 0.0), axis=1
    )
    q_scale = (q_scale * (HEAD_DIM**-0.5 * math.log2(math.e)))[:, None]
    q_start = start_of(chip_row + index)[:, None]

    w_parts, _ = lax.optimization_barrier(
        (w_out.reshape(width, shards, width).transpose(1, 0, 2), chunk)
    )
    w_column = lax.all_to_all(w_parts, REP, 0, 0, tiled=True).reshape(full_width, width)

    state = None
    for step in range(5):
        if step == 0:
            chunks, chips = [(chunk, 0)], [z]
        elif step < 4:
            chunks = [(up[step], 0), (down[step], 0)]
            chips = [(z - step) % RING, (z + step) % RING]
        else:
            chunks = [(far_low, 0), (far_high, rows)]
            chips = [(z + 4) % RING] * 2
        state = attend(
            query,
            q_scale,
            q_start,
            key_packed,
            key_scale,
            chunks,
            chips,
            [z, core],
            state,
            step == 4,
        )
    attended = state[0]
    other = core_swap(attended[1])
    mine = attended[0]
    attended = jnp.where(
        core == 0,
        jnp.concatenate([mine, other], axis=1),
        jnp.concatenate([other, mine], axis=1),
    )

    key_norm = (k_rot.astype(jnp.float32) * scales[1][:, None]).astype(jnp.bfloat16)
    my_slots = lax.dynamic_slice_in_dim(slots, first_row, rows)
    cache_sent = bucket_rows(ranks_of(my_slots), jnp.concatenate([key_norm, value], axis=1))
    cache_sent, _ = lax.optimization_barrier((cache_sent, attended))
    cached = lax.all_to_all(
        cache_sent.reshape(shards, share, 2 * width), TOK, 0, 0, tiled=True
    ).reshape(rows, 2 * width)
    slot_ids = first_row + jnp.arange(rows, dtype=jnp.int32)
    owners = jnp.arange(slots.shape[0], dtype=jnp.int32) // rows
    slot_sources = jnp.sum(
        jnp.where(slots[None, :] == slot_ids[:, None], owners[None, :], 0), axis=1
    )
    cached = place_rows(slot_sources * share + within(slot_sources), cached)

    mixed, mixed_sums = gathered_matmul(
        attended,
        [w_column],
        core,
        x,
        y,
        finish_output,
        [],
        [
            jax.ShapeDtypeStruct((rows, width), jnp.float32),
            jax.ShapeDtypeStruct((rows, 128), jnp.float32),
        ],
    )
    mixed_total = jnp.sum(spread(mixed_sums[:, :1].T, REP, 16), axis=0)[0]
    normed = mixed * lax.rsqrt(mixed_total / full_width + EPSILON)[:, None] * post_gain[None, :]
    output = (residual.astype(jnp.float32) + normed).astype(jnp.bfloat16)
    return (output, cached[:, :width], cached[:, width:])


def solution(mesh):
    grid = Mesh(mesh.devices.reshape(RING, 2, SIDE, SIDE), ("z", "core", "x", "y"))
    rows_by_features = P(TOK, REP)
    return jax.shard_map(
        body,
        mesh=grid,
        in_specs=(
            rows_by_features,
            P(None, REP),
            P(None, REP),
            P(None, REP),
            P(REP, None),
            P(REP),
            P(REP),
            P(REP),
            P(),
            P(),
            P(),
            P(),
            P(),
        ),
        out_specs=(rows_by_features,) * 3,
        check_vma=False,
    )
```

```python
import functools
import math

import jax
import jax.numpy as jnp
from jax import lax
from jax.experimental import pallas as pl
from jax.experimental.pallas import tpu as pltpu
from jax.sharding import Mesh
from jax.sharding import PartitionSpec as P

HEAD_DIM = 128
EPSILON = 1e-06
ROPE_BASE = 500000.0
SIDE = 4
RING = 8
TOK = ("z", "core")
REP = ("x", "y")
LOWEST = -1e30
FLOOR = -1e20
MATMUL_VMEM = 20 * 2**20
ATTEND_VMEM = 16 * 2**20


def plane_pairs(first, shift):
    pairs = []
    for core in range(2):
        for x in range(SIDE):
            for y in range(SIDE):
                along_x = (core == 0) == first
                to_x = (x + shift) % SIDE if along_x else x
                to_y = y if along_x else (y + shift) % SIDE
                pairs.append((core * 16 + x * 4 + y, core * 16 + to_x * 4 + to_y))
    return pairs


def plane_send(value, first, shift):
    return lax.ppermute(value, ("core", "x", "y"), plane_pairs(first, shift))


def ring_send(value, shift):
    return lax.ppermute(value, "z", [(i, (i + shift) % RING) for i in range(RING)])


def core_swap(value):
    return lax.ppermute(value, "core", [(0, 1), (1, 0)])


def spread(value, axes, size):
    copies = jnp.broadcast_to(value[None], (size, *value.shape))
    return lax.all_to_all(copies, axes, 0, 0, tiled=True)


def block_ids(steps, column, core, x, y):
    first = jnp.where(core == 0, x, y)
    second = (jnp.where(core == 0, y, x) + column) % SIDE
    mine = (first + jnp.array(steps, jnp.int32)) % SIDE
    return jnp.where(core == 0, mine * SIDE + second, second * SIDE + mine).astype(jnp.int32)


M_TILE = 512


def in_vmem(count):
    return [pl.BlockSpec(memory_space=pltpu.VMEM)] * count


def block_matmul(arrays, ids, weights, acc, finish=None, extras=(), outs=None):
    counts = [a.shape[0] for a in arrays]
    rows, depth = arrays[0].shape[1:]
    widths = [w.shape[1] for w in weights]
    total = sum(widths)
    blocks = sum(counts)
    n_arrays, n_weights, n_extras = len(arrays), len(weights), len(extras)
    has_acc = acc is not None
    if outs is None:
        outs = [jax.ShapeDtypeStruct((rows, total), jnp.float32)]

    def kernel(ids_ref, *refs):
        array_refs, refs = refs[:n_arrays], refs[n_arrays:]
        weight_refs, refs = refs[:n_weights], refs[n_weights:]
        if has_acc:
            acc_ref, refs = refs[0], refs[1:]
        extra_refs, out_refs = refs[:n_extras], refs[n_extras:]

        @pl.loop(0, rows // M_TILE)
        def _(tile):
            down = pl.ds(pl.multiple_of(tile * M_TILE, M_TILE), M_TILE)
            sums = []
            at = 0
            for w_ref, width in zip(weight_refs, widths):
                part = None
                block = 0
                for ref, count in zip(array_refs, counts):
                    for i in range(count):
                        first = pl.multiple_of(ids_ref[block] * depth, depth)
                        term = jnp.dot(
                            ref[i, down, :],
                            w_ref[pl.ds(first, depth), :],
                            preferred_element_type=jnp.float32,
                        )
                        part = term if part is None else part + term
                        block += 1
                if has_acc:
                    part = part + acc_ref[down, at : at + width]
                sums.append(part)
                at += width
            if finish is None:
                at = 0
                for part, width in zip(sums, widths):
                    out_refs[0][down, at : at + width] = part
                    at += width
            else:
                finish(sums, down, extra_refs, out_refs)

    operands = [*arrays, *weights, *([acc] if has_acc else []), *extras]
    return pl.pallas_call(
        kernel,
        grid_spec=pltpu.PrefetchScalarGridSpec(
            num_scalar_prefetch=1,
            grid=(1,),
            in_specs=in_vmem(len(operands)),
            out_specs=in_vmem(len(outs)),
        ),
        out_shape=outs,
        compiler_params=pltpu.CompilerParams(vmem_limit_bytes=MATMUL_VMEM),
        cost_estimate=pl.CostEstimate(
            flops=2 * rows * depth * total * blocks,
            bytes_accessed=blocks * depth * (rows + total) * 2 + rows * total * 8,
            transcendentals=0,
        ),
    )(ids, *operands)


def gather_features(block):
    left = plane_send(block, True, 1)
    right = plane_send(block, True, -1)
    far = plane_send(block, True, 2)
    pair = jnp.stack([block, left])
    pair_left = plane_send(pair, False, 1)
    pair_right = plane_send(pair, False, -1)
    other = jnp.stack([right, far])
    other_left = plane_send(other, False, 1)
    other_right = plane_send(other, False, -1)
    pair_far = plane_send(pair_left, False, 1)
    other_far = plane_send(other_right, False, -1)
    early = [
        (pair, [0, 3], 0),
        (other, [1, 2], 0),
        (pair_left, [0, 3], 3),
        (pair_right, [0, 3], 1),
        (other_left, [1, 2], 3),
        (other_right, [1, 2], 1),
    ]
    return early, [(pair_far, [0, 3], 2), (other_far, [1, 2], 2)]


def gathered_matmul(groups, weights, core, x, y, finish, extras, outs):
    ids = [
        jnp.concatenate([block_ids(steps, column, core, x, y) for _, steps, column in group])
        for group in groups
    ]
    early, late = ([a for a, _, _ in group] for group in groups)
    acc = block_matmul(early, ids[0], weights, None)[0]
    return block_matmul(late, ids[1], weights, acc, finish, extras, outs)


def finish_projection(parts, down, extras, outs):
    cos_ref, sin_ref, q_gain_ref, k_gain_ref = extras
    q_ref, k_ref, v_ref, sums_ref = outs
    query, key, value = parts
    q_sums = jnp.sum(query * query, axis=1, keepdims=True)
    k_sums = jnp.sum(key * key, axis=1, keepdims=True)
    lane = lax.broadcasted_iota(jnp.int32, (M_TILE, sums_ref.shape[1]), 1)
    sums_ref[down, :] = jnp.where(lane == 0, q_sums, k_sums)
    v_ref[down, :] = value.astype(jnp.bfloat16)
    cosine, sine = cos_ref[down, :], sin_ref[down, :]
    for part, gain_ref, ref in ((query, q_gain_ref, q_ref), (key, k_gain_ref, k_ref)):
        part = part * gain_ref[...]
        for head in range(2):
            at = slice(head * HEAD_DIM, (head + 1) * HEAD_DIM)
            one = part[:, at]
            ref[down, at] = one * cosine + pltpu.roll(one, HEAD_DIM // 2, 1) * sine


def output_terms(attended, w_out, core, x, y):
    rows, width = attended.shape
    ids = jnp.concatenate([block_ids([0, 1, 2, 3], column, core, x, y) for column in range(4)])

    def kernel(ids_ref, a_ref, w_ref, *out_refs):
        for i in range(16):
            first = pl.multiple_of(ids_ref[i] * width, width)
            term = jnp.dot(
                a_ref[...], w_ref[:, pl.ds(first, width)], preferred_element_type=jnp.float32
            )
            out_refs[i // 2][i % 2] = term.astype(jnp.bfloat16)

    terms = pl.pallas_call(
        kernel,
        grid_spec=pltpu.PrefetchScalarGridSpec(
            num_scalar_prefetch=1, grid=(1,), in_specs=in_vmem(2), out_specs=in_vmem(8)
        ),
        out_shape=[jax.ShapeDtypeStruct((2, rows, width), jnp.bfloat16)] * 8,
        compiler_params=pltpu.CompilerParams(vmem_limit_bytes=MATMUL_VMEM),
        cost_estimate=pl.CostEstimate(
            flops=32 * rows * width * width,
            bytes_accessed=34 * rows * width + 32 * width * width,
            transcendentals=0,
        ),
    )(ids, attended, w_out)
    return [terms[0:2], terms[2:4], terms[4:6], terms[6:8]]


def added(*terms):
    total = terms[0].astype(jnp.float32)
    for term in terms[1:]:
        total = total + term.astype(jnp.float32)
    return total


def scatter_features(terms, first_gate, second_gate):
    near, plus, far, minus = terms
    far_up = plane_send(far[0], False, 1)
    far_down = plane_send(far[1], False, -1)
    from_up = plane_send(plus[1], False, 1)
    from_down = plane_send(minus[0], False, -1)
    last_up = plane_send(added(plus[0], far_up).astype(jnp.bfloat16), False, 1)
    last_down = plane_send(added(minus[1], far_down).astype(jnp.bfloat16), False, -1)
    last_up, last_down, first_gate = lax.optimization_barrier((last_up, last_down, first_gate))
    second = second_gate(first_gate)

    def part(i):
        if i < 2:
            return added(near[0][i], from_down[i], last_up[i])
        return added(near[1][i - 2], from_up[i - 2], last_down[i - 2])

    sent = [
        plane_send(part(i).astype(jnp.bfloat16), True, shift)
        for i, shift in ((1, 1), (2, 2), (3, -1))
    ]
    *sent, second = lax.optimization_barrier((*sent, second))
    return part(0) + added(*sent), second


Q_TILE = 512
K_TILE = 512


def attend(query, q_start, key_packed, chunks, chips, place, state, last):
    rows = query.shape[0]
    n_chunks = len(chunks)
    has_state = state is not None
    lanes = key_packed.shape[1]
    per_chip = rows // lanes
    tiles = rows // Q_TILE

    def kernel(ids_ref, *refs):
        q_ref, start_ref, kp_ref, *refs = refs
        chunk_refs, refs = refs[:n_chunks], refs[n_chunks:]
        if has_state:
            top_in, total_in, sum_in, *refs = refs
        chip_at, core = ids_ref[n_chunks], ids_ref[n_chunks + 1]
        q_tile = q_ref[...]
        start = start_ref[...]
        packed = (
            chip_at * rows
            + pl.program_id(0) * Q_TILE
            + lax.broadcasted_iota(jnp.int32, (1, Q_TILE), 1)
        )
        if has_state:
            top, total, weighted = top_in[:1, :], total_in[:1, :], sum_in[...]
        else:
            top = jnp.full((1, Q_TILE), FLOOR, jnp.float32)
            total = jnp.zeros((1, Q_TILE), jnp.float32)
            weighted = jnp.zeros((HEAD_DIM, Q_TILE), jnp.float32)
        for i, (ref, (array, first)) in enumerate(zip(chunk_refs, chunks)):
            for at in range(0, array.shape[0], K_TILE):
                keys = ref[at : at + K_TILE, :HEAD_DIM]
                values = ref[at : at + K_TILE, HEAD_DIM:]
                columns = []
                for k in range(K_TILE // lanes):
                    group = (first + at) // lanes + k
                    row = lax.rem(group + core * (per_chip // 2), per_chip)
                    line = kp_ref[pl.ds(ids_ref[i] * per_chip + row, 1), :]
                    columns.append(jnp.broadcast_to(line, (lanes, lanes)).T)
                kp = jnp.concatenate(columns, axis=0)
                kp = jnp.concatenate([kp] * (Q_TILE // lanes), axis=1)
                scores = lax.dot_general(
                    keys, q_tile, (((1,), (1,)), ((), ())), preferred_element_type=jnp.float32
                )
                allowed = (kp <= packed) & (kp >= start)
                scores = jnp.where(allowed, scores, LOWEST)
                new_top = jnp.maximum(top, jnp.max(scores, axis=0, keepdims=True))
                weights = jnp.exp2(scores - new_top)
                factor = jnp.exp2(top - new_top)
                total = total * factor + jnp.sum(weights, axis=0, keepdims=True)
                weighted = weighted * factor + lax.dot_general(
                    values,
                    weights.astype(jnp.bfloat16),
                    (((0,), (0,)), ((), ())),
                    preferred_element_type=jnp.float32,
                )
                top = new_top
        if last:
            refs[0][0] = (weighted / total).T.astype(jnp.bfloat16)
        else:
            top_out, total_out, sum_out = refs
            top_out[...] = jnp.broadcast_to(top, top_out.shape)
            total_out[...] = jnp.broadcast_to(total, total_out.shape)
            sum_out[...] = weighted

    def across(height):
        return pl.BlockSpec((height, Q_TILE), lambda i, ids_ref: (0, i))

    in_specs = [pl.BlockSpec((Q_TILE, HEAD_DIM), lambda i, ids_ref: (i, 0)), across(1)]
    in_specs += in_vmem(1 + n_chunks)
    operands = [query, q_start, key_packed, *[a for a, _ in chunks]]
    if has_state:
        in_specs += [across(8), across(8), across(HEAD_DIM)]
        operands += list(state)
    if last:
        out_shape = [jax.ShapeDtypeStruct((tiles, Q_TILE, HEAD_DIM), jnp.bfloat16)]
        out_specs = [
            pl.BlockSpec(
                (1, Q_TILE, HEAD_DIM),
                lambda i, ids_ref: (lax.rem(i + ids_ref[n_chunks + 1], tiles), 0, 0),
            )
        ]
    else:
        out_shape = [jax.ShapeDtypeStruct((8, rows), jnp.float32)] * 2
        out_shape.append(jax.ShapeDtypeStruct((HEAD_DIM, rows), jnp.float32))
        out_specs = [across(8), across(8), across(HEAD_DIM)]
    keys_seen = sum(a.shape[0] for a, _ in chunks)
    ids = jnp.concatenate([jnp.stack(chips), jnp.stack(place)]).astype(jnp.int32)
    return pl.pallas_call(
        kernel,
        grid_spec=pltpu.PrefetchScalarGridSpec(
            num_scalar_prefetch=1,
            grid=(tiles,),
            in_specs=in_specs,
            out_specs=out_specs,
        ),
        out_shape=out_shape,
        compiler_params=pltpu.CompilerParams(vmem_limit_bytes=ATTEND_VMEM),
        cost_estimate=pl.CostEstimate(
            flops=4 * rows * keys_seen * HEAD_DIM,
            bytes_accessed=rows * HEAD_DIM * 10 + keys_seen * 1024,
            transcendentals=0,
        ),
    )(ids, *operands)


C_TILE = 256


def pick_rows(chunks, chips, slot_lines, core, row_base, acc, last):
    n_chunks = len(chunks)
    lanes = slot_lines.shape[1]
    rows = 2 * K_TILE
    per_chip = rows // lanes
    width = chunks[0][0].shape[1]
    has_acc = acc is not None

    def kernel(ids_ref, lines_ref, *refs):
        chunk_refs, refs = refs[:n_chunks], refs[n_chunks:]
        tile = pl.program_id(0)
        mine = (
            ids_ref[n_chunks + 1] + tile * C_TILE + lax.broadcasted_iota(jnp.int32, (C_TILE, 1), 0)
        )
        total = refs[0][...] if has_acc else jnp.zeros((C_TILE, width), jnp.float32)
        for i, (ref, (array, first)) in enumerate(zip(chunk_refs, chunks)):
            for at in range(0, array.shape[0], K_TILE):
                chosen = []
                for k in range(K_TILE // lanes):
                    group = (first + at) // lanes + k
                    row = lax.rem(group + ids_ref[n_chunks] * (per_chip // 2), per_chip)
                    line = lines_ref[pl.ds(ids_ref[i] * per_chip + row, 1), :]
                    chosen.append(jnp.where(line == mine, 1.0, 0.0).astype(jnp.bfloat16))
                total = total + jnp.dot(
                    jnp.concatenate(chosen, axis=1),
                    ref[at : at + K_TILE, :],
                    preferred_element_type=jnp.float32,
                )
        refs[-1][...] = total.astype(refs[-1].dtype)

    def tile_spec():
        return pl.BlockSpec((C_TILE, width), lambda i, ids_ref: (i, 0))

    operands = [slot_lines, *[a for a, _ in chunks], *([acc] if has_acc else [])]
    ids = jnp.stack([*chips, core, row_base]).astype(jnp.int32)
    keys_seen = sum(a.shape[0] for a, _ in chunks)
    return pl.pallas_call(
        kernel,
        grid_spec=pltpu.PrefetchScalarGridSpec(
            num_scalar_prefetch=1,
            grid=(rows // C_TILE,),
            in_specs=in_vmem(1 + n_chunks) + ([tile_spec()] if has_acc else []),
            out_specs=[tile_spec()],
        ),
        out_shape=[jax.ShapeDtypeStruct((rows, width), jnp.bfloat16 if last else jnp.float32)],
        compiler_params=pltpu.CompilerParams(vmem_limit_bytes=ATTEND_VMEM),
        cost_estimate=pl.CostEstimate(
            flops=2 * rows * keys_seen * width,
            bytes_accessed=rows * width * 6 + keys_seen * width * 2,
            transcendentals=0,
        ),
    )(ids, *operands)[0]


def ranks_of(values):
    return jnp.sum((values[None, :] < values[:, None]).astype(jnp.int32), axis=1)


def within(sources):
    index = jnp.arange(sources.shape[0], dtype=jnp.int32)
    same = (sources[None, :] == sources[:, None]) & (index[None, :] < index[:, None])
    return jnp.sum(same.astype(jnp.int32), axis=1)


def place_rows(positions, rows):
    index = jnp.arange(rows.shape[0], dtype=jnp.int32)
    chosen = (positions[:, None] == index[None, :]).astype(jnp.bfloat16)
    return jnp.dot(chosen, rows, preferred_element_type=jnp.float32).astype(jnp.bfloat16)


def bucket_rows(ranks, rows):
    index = jnp.arange(rows.shape[0], dtype=jnp.int32)
    chosen = (ranks[None, :] == index[:, None]).astype(jnp.bfloat16)
    return jnp.dot(chosen, rows, preferred_element_type=jnp.float32).astype(jnp.bfloat16)


def body(
    hidden_in,
    w_query,
    w_key,
    w_value,
    w_out,
    q_gain,
    k_gain,
    post_gain,
    prompt_lengths,
    segment_ids,
    deal,
    inverse,
    slots,
):
    rows, width = hidden_in.shape
    full_width = w_query.shape[0]
    shards = 16
    share = rows // shards
    x, y = lax.axis_index("x"), lax.axis_index("y")
    z, core = lax.axis_index("z"), lax.axis_index("core")
    first_row = (z * 2 + core) * rows
    chip_row = z * 2 * rows

    prompt_ids = jnp.arange(prompt_lengths.shape[0], dtype=jnp.int32)
    prompt_starts = jnp.sum(
        jnp.where(prompt_ids[None, :] < prompt_ids[:, None], prompt_lengths[None, :], 0), axis=1
    )

    def start_of(packed):
        return jnp.max(
            jnp.where(prompt_starts[None, :] <= packed[:, None], prompt_starts[None, :], 0), axis=1
        )

    my_packed = lax.dynamic_slice_in_dim(deal, first_row, rows)
    positions = (my_packed - start_of(my_packed)).astype(jnp.float32)
    half = HEAD_DIM // 2
    frequency = ROPE_BASE ** (-jnp.arange(half, dtype=jnp.float32) * 2.0 / HEAD_DIM)
    angles = positions[:, None] * frequency[None, :]
    cosine, sine = jnp.cos(angles), jnp.sin(angles)
    cosine = jnp.concatenate([cosine, cosine], axis=1)
    sine = jnp.concatenate([-sine, sine], axis=1)

    ranks = ranks_of(my_packed)
    groups = gather_features(hidden_in)
    float_rows = jax.ShapeDtypeStruct((rows, width), jnp.float32)
    half_rows = jax.ShapeDtypeStruct((rows, width), jnp.bfloat16)
    lane_rows = jax.ShapeDtypeStruct((rows, 128), jnp.float32)
    q_rot, k_rot, value, sums = gathered_matmul(
        groups,
        [w_query, w_key, w_value],
        core,
        x,
        y,
        finish_projection,
        [cosine, sine, q_gain[None, :], k_gain[None, :]],
        [float_rows, float_rows, half_rows, lane_rows],
    )

    all_sums = jnp.sum(spread(sums[:, :2].T, REP, 16), axis=0)
    scales = lax.rsqrt(all_sums / full_width + EPSILON)
    to_scores = HEAD_DIM**-0.5 * math.log2(math.e)
    q_half = (q_rot * (scales[0] * to_scores)[:, None]).astype(jnp.bfloat16)
    k_half = (k_rot * scales[1][:, None]).astype(jnp.bfloat16)

    def own_head(both):
        return jnp.where(core == 0, both[:, :HEAD_DIM], both[:, HEAD_DIM:])

    def other_head(both):
        return jnp.where(core == 0, both[:, HEAD_DIM:], both[:, :HEAD_DIM])

    kept = jnp.concatenate([own_head(k_half), own_head(value)], axis=1)
    given = jnp.concatenate([other_head(k_half), other_head(value)], axis=1)
    chunk = jnp.concatenate([kept, core_swap(given)])

    up, down = [chunk], [chunk]
    q_ready = q_half
    for step in range(3):
        up.append(ring_send(up[-1], 1))
        down.append(ring_send(down[-1], -1))
        if step == 0:
            up[1], down[1], q_ready = lax.optimization_barrier((up[1], down[1], q_ready))
    key_packed = deal.reshape(-1, 128)

    bucketed = bucket_rows(ranks, jnp.concatenate([q_ready, hidden_in], axis=1))
    q_sent = bucketed[:, :width].reshape(RING, 2 * share, 2, HEAD_DIM)
    q_sent = q_sent.transpose(0, 2, 1, 3).reshape(shards, share, 2 * HEAD_DIM)
    h_sent = bucketed[:, width:].reshape(shards, share, width)
    moved = lax.all_to_all(jnp.concatenate([q_sent, h_sent], axis=2), TOK, 0, 0, tiled=True)
    sources = lax.dynamic_slice_in_dim(inverse, chip_row, 2 * rows) // rows
    q_places = sources * (2 * share) + within(sources)
    query = place_rows(q_places, moved[:, :, :width].reshape(2 * rows, HEAD_DIM))
    my_sources = lax.dynamic_slice_in_dim(inverse, first_row, rows) // rows
    residual = place_rows(
        my_sources * share + within(my_sources), moved[:, :, width:].reshape(rows, width)
    )
    q_start = start_of(chip_row + jnp.arange(2 * rows, dtype=jnp.int32))[None, :]

    place = [z, core]
    state = attend(
        query,
        q_start,
        key_packed,
        [(chunk, 0), (up[1], 0), (down[1], 0)],
        [z, (z - 1) % RING, (z + 1) % RING],
        place,
        None,
        False,
    )
    up[3], down[3], *state = lax.optimization_barrier((up[3], down[3], *state))
    far_low = ring_send(up[3][:rows], 1)
    far_high = ring_send(down[3][rows:], -1)
    state = attend(
        query,
        q_start,
        key_packed,
        [(up[2], 0), (down[2], 0)],
        [(z - 2) % RING, (z + 2) % RING],
        place,
        state,
        False,
    )
    state = attend(
        query,
        q_start,
        key_packed,
        [(up[3], 0), (down[3], 0)],
        [(z - 3) % RING, (z + 3) % RING],
        place,
        state,
        False,
    )
    state = attend(
        query,
        q_start,
        key_packed,
        [(far_low, 0), (far_high, rows)],
        [(z + 4) % RING] * 2,
        place,
        state,
        True,
    )
    attended = state[0]
    other = core_swap(attended[1])
    mine = attended[0]
    attended = jnp.where(
        core == 0,
        jnp.concatenate([mine, other], axis=1),
        jnp.concatenate([other, mine], axis=1),
    )

    slot_lines = slots.reshape(-1, 128)
    chosen = pick_rows(
        [(chunk, 0), (up[1], 0), (down[1], 0), (up[2], 0)],
        [z, (z - 1) % RING, (z + 1) % RING, (z - 2) % RING],
        slot_lines,
        core,
        chip_row,
        None,
        False,
    )
    pick_rest = functools.partial(
        pick_rows,
        [(down[2], 0), (up[3], 0), (down[3], 0), (far_low, 0), (far_high, rows)],
        [(z + 2) % RING, (z - 3) % RING, (z + 3) % RING, (z + 4) % RING, (z + 4) % RING],
        slot_lines,
        core,
        chip_row,
        last=True,
    )
    terms = output_terms(attended, w_out, core, x, y)
    mixed, chosen = scatter_features(terms, chosen, lambda before: pick_rest(acc=before))
    kept = jnp.where(core == 0, chosen[:rows], chosen[rows:])
    taken = core_swap(jnp.where(core == 0, chosen[rows:], chosen[:rows]))

    def by_head(at):
        own, swapped = kept[:, at : at + HEAD_DIM], taken[:, at : at + HEAD_DIM]
        low, high = jnp.where(core == 0, own, swapped), jnp.where(core == 0, swapped, own)
        return jnp.concatenate([low, high], axis=1)

    cache_keys, cache_values = by_head(0), by_head(HEAD_DIM)

    mixed_total = jnp.sum(spread(jnp.sum(mixed * mixed, axis=1)[None, :], REP, 16), axis=0)[0]
    normed = mixed * lax.rsqrt(mixed_total / full_width + EPSILON)[:, None] * post_gain[None, :]
    output = (residual.astype(jnp.float32) + normed).astype(jnp.bfloat16)
    return (output, cache_keys, cache_values)


def solution(mesh):
    grid = Mesh(mesh.devices.reshape(RING, 2, SIDE, SIDE), ("z", "core", "x", "y"))
    rows_by_features = P(TOK, REP)
    return jax.shard_map(
        body,
        mesh=grid,
        in_specs=(
            rows_by_features,
            P(None, REP),
            P(None, REP),
            P(None, REP),
            P(REP, None),
            P(REP),
            P(REP),
            P(REP),
            P(),
            P(),
            P(),
            P(),
            P(),
        ),
        out_specs=(rows_by_features,) * 3,
        check_vma=False,
    )
```

```python
import functools
import math

import jax
import jax.numpy as jnp
from jax import lax
from jax.experimental import pallas as pl
from jax.experimental.pallas import tpu as pltpu
from jax.sharding import Mesh
from jax.sharding import PartitionSpec as P

HEAD_DIM = 128
EPSILON = 1e-06
ROPE_BASE = 500000.0
SIDE = 4
RING = 8
TOK = ("z", "core")
REP = ("x", "y")
LOWEST = -1e30
FLOOR = -1e20
MATMUL_VMEM = 20 * 2**20
ATTEND_VMEM = 16 * 2**20


def plane_pairs(first, shift):
    pairs = []
    for core in range(2):
        for x in range(SIDE):
            for y in range(SIDE):
                along_x = (core == 0) == first
                to_x = (x + shift) % SIDE if along_x else x
                to_y = y if along_x else (y + shift) % SIDE
                pairs.append((core * 16 + x * 4 + y, core * 16 + to_x * 4 + to_y))
    return pairs


def plane_send(value, first, shift):
    return lax.ppermute(value, ("core", "x", "y"), plane_pairs(first, shift))


def ring_send(value, shift):
    return lax.ppermute(value, "z", [(i, (i + shift) % RING) for i in range(RING)])


def core_swap(value):
    return lax.ppermute(value, "core", [(0, 1), (1, 0)])


def spread(value, axes, size):
    copies = jnp.broadcast_to(value[None], (size, *value.shape))
    return lax.all_to_all(copies, axes, 0, 0, tiled=True)


def block_ids(steps, column, core, x, y):
    first = jnp.where(core == 0, x, y)
    second = (jnp.where(core == 0, y, x) + column) % SIDE
    mine = (first + jnp.array(steps, jnp.int32)) % SIDE
    return jnp.where(core == 0, mine * SIDE + second, second * SIDE + mine).astype(jnp.int32)


M_TILE = 512


def in_vmem(count):
    return [pl.BlockSpec(memory_space=pltpu.VMEM)] * count


def block_matmul(arrays, ids, weights, acc, finish=None, extras=(), outs=None):
    counts = [a.shape[0] for a in arrays]
    rows, depth = arrays[0].shape[1:]
    widths = [w.shape[1] for w in weights]
    total = sum(widths)
    blocks = sum(counts)
    n_arrays, n_weights, n_extras = len(arrays), len(weights), len(extras)
    has_acc = acc is not None
    if outs is None:
        outs = [jax.ShapeDtypeStruct((rows, total), jnp.float32)]

    def kernel(ids_ref, *refs):
        array_refs, refs = refs[:n_arrays], refs[n_arrays:]
        weight_refs, refs = refs[:n_weights], refs[n_weights:]
        if has_acc:
            acc_ref, refs = refs[0], refs[1:]
        extra_refs, out_refs = refs[:n_extras], refs[n_extras:]

        @pl.loop(0, rows // M_TILE)
        def _(tile):
            down = pl.ds(pl.multiple_of(tile * M_TILE, M_TILE), M_TILE)
            sums = []
            at = 0
            for w_ref, width in zip(weight_refs, widths):
                part = None
                block = 0
                for ref, count in zip(array_refs, counts):
                    for i in range(count):
                        first = pl.multiple_of(ids_ref[block] * depth, depth)
                        term = jnp.dot(
                            ref[i, down, :],
                            w_ref[pl.ds(first, depth), :],
                            preferred_element_type=jnp.float32,
                        )
                        part = term if part is None else part + term
                        block += 1
                if has_acc:
                    part = part + acc_ref[down, at : at + width]
                sums.append(part)
                at += width
            if finish is None:
                at = 0
                for part, width in zip(sums, widths):
                    out_refs[0][down, at : at + width] = part
                    at += width
            else:
                finish(sums, down, extra_refs, out_refs)

    operands = [*arrays, *weights, *([acc] if has_acc else []), *extras]
    return pl.pallas_call(
        kernel,
        grid_spec=pltpu.PrefetchScalarGridSpec(
            num_scalar_prefetch=1,
            grid=(1,),
            in_specs=in_vmem(len(operands)),
            out_specs=in_vmem(len(outs)),
        ),
        out_shape=outs,
        compiler_params=pltpu.CompilerParams(vmem_limit_bytes=MATMUL_VMEM),
        cost_estimate=pl.CostEstimate(
            flops=2 * rows * depth * total * blocks,
            bytes_accessed=blocks * depth * (rows + total) * 2 + rows * total * 8,
            transcendentals=0,
        ),
    )(ids, *operands)


def gather_features(block):
    left = plane_send(block, True, 1)
    right = plane_send(block, True, -1)
    far = plane_send(block, True, 2)
    pair = jnp.stack([block, left])
    pair_left = plane_send(pair, False, 1)
    pair_right = plane_send(pair, False, -1)
    other = jnp.stack([right, far])
    other_left = plane_send(other, False, 1)
    other_right = plane_send(other, False, -1)
    pair_far = plane_send(pair_left, False, 1)
    other_far = plane_send(other_right, False, -1)
    early = [
        (pair, [0, 3], 0),
        (other, [1, 2], 0),
        (pair_left, [0, 3], 3),
        (pair_right, [0, 3], 1),
        (other_left, [1, 2], 3),
        (other_right, [1, 2], 1),
    ]
    return early, [(pair_far, [0, 3], 2), (other_far, [1, 2], 2)]


def gathered_matmul(groups, weights, core, x, y, finish, extras, outs):
    ids = [
        jnp.concatenate([block_ids(steps, column, core, x, y) for _, steps, column in group])
        for group in groups
    ]
    early, late = ([a for a, _, _ in group] for group in groups)
    acc = block_matmul(early, ids[0], weights, None)[0]
    return block_matmul(late, ids[1], weights, acc, finish, extras, outs)


def finish_projection(parts, down, extras, outs):
    cos_ref, sin_ref, q_gain_ref, k_gain_ref = extras
    q_ref, k_ref, v_ref, sums_ref = outs
    query, key, value = parts
    q_sums = jnp.sum(query * query, axis=1, keepdims=True)
    k_sums = jnp.sum(key * key, axis=1, keepdims=True)
    lane = lax.broadcasted_iota(jnp.int32, (M_TILE, sums_ref.shape[1]), 1)
    sums_ref[down, :] = jnp.where(lane == 0, q_sums, k_sums)
    v_ref[down, :] = value.astype(jnp.bfloat16)
    cosine, sine = cos_ref[down, :], sin_ref[down, :]
    for part, gain_ref, ref in ((query, q_gain_ref, q_ref), (key, k_gain_ref, k_ref)):
        part = part * gain_ref[...]
        for head in range(2):
            at = slice(head * HEAD_DIM, (head + 1) * HEAD_DIM)
            one = part[:, at]
            ref[down, at] = one * cosine + pltpu.roll(one, HEAD_DIM // 2, 1) * sine


TERM_PLACE = ((0, 0), (0, 2), (3, 0), (1, 2), (1, 0), (2, 0), (2, 2), (4, 0))


def output_terms(attended, w_out, core, x, y):
    rows, width = attended.shape
    ids = jnp.concatenate([block_ids([0, 1, 2, 3], column, core, x, y) for column in range(4)])

    def kernel(ids_ref, a_ref, w_ref, *out_refs):
        for i in range(16):
            first = pl.multiple_of(ids_ref[i] * width, width)
            term = jnp.dot(
                a_ref[...], w_ref[:, pl.ds(first, width)], preferred_element_type=jnp.float32
            )
            out_refs[TERM_PLACE[i // 2][0]][TERM_PLACE[i // 2][1] + i % 2] = term.astype(jnp.bfloat16)

    return pl.pallas_call(
        kernel,
        grid_spec=pltpu.PrefetchScalarGridSpec(
            num_scalar_prefetch=1, grid=(1,), in_specs=in_vmem(2), out_specs=in_vmem(5)
        ),
        out_shape=[jax.ShapeDtypeStruct((n, rows, width), jnp.bfloat16) for n in (4, 4, 4, 2, 2)],
        compiler_params=pltpu.CompilerParams(vmem_limit_bytes=MATMUL_VMEM),
        cost_estimate=pl.CostEstimate(
            flops=32 * rows * width * width,
            bytes_accessed=34 * rows * width + 32 * width * width,
            transcendentals=0,
        ),
    )(ids, attended, w_out)


def added(*terms):
    total = terms[0].astype(jnp.float32)
    for term in terms[1:]:
        total = total + term.astype(jnp.float32)
    return total


def scatter_features(terms, first_gate, second_gate):
    near, up, down, plus, minus = terms
    from_up = plane_send(up, False, 1)
    from_down = plane_send(down, False, -1)
    last_up = plane_send(added(plus, from_up[:2]).astype(jnp.bfloat16), False, 1)
    last_down = plane_send(added(minus, from_down[:2]).astype(jnp.bfloat16), False, -1)
    last_up, last_down, first_gate = lax.optimization_barrier((last_up, last_down, first_gate))
    second = second_gate(first_gate)

    def part(i):
        if i < 2:
            return added(near[i], from_down[2 + i], last_up[i])
        return added(near[i], from_up[i], last_down[i - 2])

    sent = [
        plane_send(part(i).astype(jnp.bfloat16), True, shift)
        for i, shift in ((1, 1), (2, 2), (3, -1))
    ]
    *sent, second = lax.optimization_barrier((*sent, second))
    return part(0) + added(*sent), second


Q_TILE = 512
K_TILE = 512


def attend(query, q_start, key_packed, chunks, chips, place, state, last):
    rows = query.shape[0]
    n_chunks = len(chunks)
    has_state = state is not None
    lanes = key_packed.shape[1]
    per_chip = rows // lanes
    tiles = rows // Q_TILE

    def kernel(ids_ref, *refs):
        q_ref, start_ref, kp_ref, *refs = refs
        chunk_refs, refs = refs[:n_chunks], refs[n_chunks:]
        if has_state:
            top_in, total_in, sum_in, *refs = refs
        chip_at, core = ids_ref[n_chunks], ids_ref[n_chunks + 1]
        q_tile = q_ref[...]
        start = start_ref[...]
        packed = (
            chip_at * rows
            + pl.program_id(0) * Q_TILE
            + lax.broadcasted_iota(jnp.int32, (1, Q_TILE), 1)
        )
        if has_state:
            top, total, weighted = top_in[:1, :], total_in[:1, :], sum_in[...]
        else:
            top = jnp.full((1, Q_TILE), FLOOR, jnp.float32)
            total = jnp.zeros((1, Q_TILE), jnp.float32)
            weighted = jnp.zeros((HEAD_DIM, Q_TILE), jnp.float32)
        for i, (ref, (array, first)) in enumerate(zip(chunk_refs, chunks)):
            for at in range(0, array.shape[0], K_TILE):
                keys = ref[at : at + K_TILE, :HEAD_DIM]
                values = ref[at : at + K_TILE, HEAD_DIM:]
                columns = []
                for k in range(K_TILE // lanes):
                    group = (first + at) // lanes + k
                    row = lax.rem(group + core * (per_chip // 2), per_chip)
                    line = kp_ref[pl.ds(ids_ref[i] * per_chip + row, 1), :]
                    columns.append(jnp.broadcast_to(line, (lanes, lanes)).T)
                kp = jnp.concatenate(columns, axis=0)
                kp = jnp.concatenate([kp] * (Q_TILE // lanes), axis=1)
                scores = lax.dot_general(
                    keys, q_tile, (((1,), (1,)), ((), ())), preferred_element_type=jnp.float32
                )
                allowed = (kp <= packed) & (kp >= start)
                scores = jnp.where(allowed, scores, LOWEST)
                new_top = jnp.maximum(top, jnp.max(scores, axis=0, keepdims=True))
                weights = jnp.exp2(scores - new_top)
                factor = jnp.exp2(top - new_top)
                total = total * factor + jnp.sum(weights, axis=0, keepdims=True)
                weighted = weighted * factor + lax.dot_general(
                    values,
                    weights.astype(jnp.bfloat16),
                    (((0,), (0,)), ((), ())),
                    preferred_element_type=jnp.float32,
                )
                top = new_top
        if last:
            refs[0][0] = (weighted / total).T.astype(jnp.bfloat16)
        else:
            top_out, total_out, sum_out = refs
            top_out[...] = jnp.broadcast_to(top, top_out.shape)
            total_out[...] = jnp.broadcast_to(total, total_out.shape)
            sum_out[...] = weighted

    def across(height):
        return pl.BlockSpec((height, Q_TILE), lambda i, ids_ref: (0, i))

    in_specs = [pl.BlockSpec((Q_TILE, HEAD_DIM), lambda i, ids_ref: (i, 0)), across(1)]
    in_specs += in_vmem(1 + n_chunks)
    operands = [query, q_start, key_packed, *[a for a, _ in chunks]]
    if has_state:
        in_specs += [across(8), across(8), across(HEAD_DIM)]
        operands += list(state)
    if last:
        out_shape = [jax.ShapeDtypeStruct((tiles, Q_TILE, HEAD_DIM), jnp.bfloat16)]
        out_specs = [
            pl.BlockSpec(
                (1, Q_TILE, HEAD_DIM),
                lambda i, ids_ref: (lax.rem(i + ids_ref[n_chunks + 1], tiles), 0, 0),
            )
        ]
    else:
        out_shape = [jax.ShapeDtypeStruct((8, rows), jnp.float32)] * 2
        out_shape.append(jax.ShapeDtypeStruct((HEAD_DIM, rows), jnp.float32))
        out_specs = [across(8), across(8), across(HEAD_DIM)]
    keys_seen = sum(a.shape[0] for a, _ in chunks)
    ids = jnp.concatenate([jnp.stack(chips), jnp.stack(place)]).astype(jnp.int32)
    return pl.pallas_call(
        kernel,
        grid_spec=pltpu.PrefetchScalarGridSpec(
            num_scalar_prefetch=1,
            grid=(tiles,),
            in_specs=in_specs,
            out_specs=out_specs,
        ),
        out_shape=out_shape,
        compiler_params=pltpu.CompilerParams(vmem_limit_bytes=ATTEND_VMEM),
        cost_estimate=pl.CostEstimate(
            flops=4 * rows * keys_seen * HEAD_DIM,
            bytes_accessed=rows * HEAD_DIM * 10 + keys_seen * 1024,
            transcendentals=0,
        ),
    )(ids, *operands)


C_TILE = 256


def pick_rows(chunks, chips, slot_lines, core, row_base, acc, last):
    n_chunks = len(chunks)
    lanes = slot_lines.shape[1]
    rows = 2 * K_TILE
    per_chip = rows // lanes
    width = chunks[0][0].shape[1]
    has_acc = acc is not None

    def kernel(ids_ref, lines_ref, *refs):
        chunk_refs, refs = refs[:n_chunks], refs[n_chunks:]
        tile = pl.program_id(0)
        mine = (
            ids_ref[n_chunks + 1] + tile * C_TILE + lax.broadcasted_iota(jnp.int32, (C_TILE, 1), 0)
        )
        total = refs[0][...] if has_acc else jnp.zeros((C_TILE, width), jnp.float32)
        for i, (ref, (array, first)) in enumerate(zip(chunk_refs, chunks)):
            for at in range(0, array.shape[0], K_TILE):
                chosen = []
                for k in range(K_TILE // lanes):
                    group = (first + at) // lanes + k
                    row = lax.rem(group + ids_ref[n_chunks] * (per_chip // 2), per_chip)
                    line = lines_ref[pl.ds(ids_ref[i] * per_chip + row, 1), :]
                    chosen.append(jnp.where(line == mine, 1.0, 0.0).astype(jnp.bfloat16))
                total = total + jnp.dot(
                    jnp.concatenate(chosen, axis=1),
                    ref[at : at + K_TILE, :],
                    preferred_element_type=jnp.float32,
                )
        refs[-1][...] = total.astype(refs[-1].dtype)

    def tile_spec():
        return pl.BlockSpec((C_TILE, width), lambda i, ids_ref: (i, 0))

    operands = [slot_lines, *[a for a, _ in chunks], *([acc] if has_acc else [])]
    ids = jnp.stack([*chips, core, row_base]).astype(jnp.int32)
    keys_seen = sum(a.shape[0] for a, _ in chunks)
    return pl.pallas_call(
        kernel,
        grid_spec=pltpu.PrefetchScalarGridSpec(
            num_scalar_prefetch=1,
            grid=(rows // C_TILE,),
            in_specs=in_vmem(1 + n_chunks) + ([tile_spec()] if has_acc else []),
            out_specs=[tile_spec()],
        ),
        out_shape=[jax.ShapeDtypeStruct((rows, width), jnp.bfloat16 if last else jnp.float32)],
        compiler_params=pltpu.CompilerParams(vmem_limit_bytes=ATTEND_VMEM),
        cost_estimate=pl.CostEstimate(
            flops=2 * rows * keys_seen * width,
            bytes_accessed=rows * width * 6 + keys_seen * width * 2,
            transcendentals=0,
        ),
    )(ids, *operands)[0]


def ranks_of(values):
    return jnp.sum((values[None, :] < values[:, None]).astype(jnp.int32), axis=1)


def within(sources):
    index = jnp.arange(sources.shape[0], dtype=jnp.int32)
    same = (sources[None, :] == sources[:, None]) & (index[None, :] < index[:, None])
    return jnp.sum(same.astype(jnp.int32), axis=1)


def place_rows(positions, rows):
    index = jnp.arange(rows.shape[0], dtype=jnp.int32)
    chosen = (positions[:, None] == index[None, :]).astype(jnp.bfloat16)
    return jnp.dot(chosen, rows, preferred_element_type=jnp.float32).astype(jnp.bfloat16)


def bucket_rows(ranks, rows):
    index = jnp.arange(rows.shape[0], dtype=jnp.int32)
    chosen = (ranks[None, :] == index[:, None]).astype(jnp.bfloat16)
    return jnp.dot(chosen, rows, preferred_element_type=jnp.float32).astype(jnp.bfloat16)


def body(
    hidden_in,
    w_query,
    w_key,
    w_value,
    w_out,
    q_gain,
    k_gain,
    post_gain,
    prompt_lengths,
    segment_ids,
    deal,
    inverse,
    slots,
):
    rows, width = hidden_in.shape
    full_width = w_query.shape[0]
    shards = 16
    share = rows // shards
    x, y = lax.axis_index("x"), lax.axis_index("y")
    z, core = lax.axis_index("z"), lax.axis_index("core")
    first_row = (z * 2 + core) * rows
    chip_row = z * 2 * rows

    prompt_ids = jnp.arange(prompt_lengths.shape[0], dtype=jnp.int32)
    prompt_starts = jnp.sum(
        jnp.where(prompt_ids[None, :] < prompt_ids[:, None], prompt_lengths[None, :], 0), axis=1
    )

    def start_of(packed):
        return jnp.max(
            jnp.where(prompt_starts[None, :] <= packed[:, None], prompt_starts[None, :], 0), axis=1
        )

    my_packed = lax.dynamic_slice_in_dim(deal, first_row, rows)
    positions = (my_packed - start_of(my_packed)).astype(jnp.float32)
    half = HEAD_DIM // 2
    frequency = ROPE_BASE ** (-jnp.arange(half, dtype=jnp.float32) * 2.0 / HEAD_DIM)
    angles = positions[:, None] * frequency[None, :]
    cosine, sine = jnp.cos(angles), jnp.sin(angles)
    cosine = jnp.concatenate([cosine, cosine], axis=1)
    sine = jnp.concatenate([-sine, sine], axis=1)

    ranks = ranks_of(my_packed)
    groups = gather_features(hidden_in)
    float_rows = jax.ShapeDtypeStruct((rows, width), jnp.float32)
    half_rows = jax.ShapeDtypeStruct((rows, width), jnp.bfloat16)
    lane_rows = jax.ShapeDtypeStruct((rows, 128), jnp.float32)
    q_rot, k_rot, value, sums = gathered_matmul(
        groups,
        [w_query, w_key, w_value],
        core,
        x,
        y,
        finish_projection,
        [cosine, sine, q_gain[None, :], k_gain[None, :]],
        [float_rows, float_rows, half_rows, lane_rows],
    )

    all_sums = jnp.sum(spread(sums[:, :2].T, REP, 16), axis=0)
    scales = lax.rsqrt(all_sums / full_width + EPSILON)
    to_scores = HEAD_DIM**-0.5 * math.log2(math.e)
    q_half = (q_rot * (scales[0] * to_scores)[:, None]).astype(jnp.bfloat16)
    k_half = (k_rot * scales[1][:, None]).astype(jnp.bfloat16)

    def own_head(both):
        return jnp.where(core == 0, both[:, :HEAD_DIM], both[:, HEAD_DIM:])

    def other_head(both):
        return jnp.where(core == 0, both[:, HEAD_DIM:], both[:, :HEAD_DIM])

    kept = jnp.concatenate([own_head(k_half), own_head(value)], axis=1)
    given = jnp.concatenate([other_head(k_half), other_head(value)], axis=1)
    chunk = jnp.concatenate([kept, core_swap(given)])

    up, down = [chunk], [chunk]
    for _ in range(3):
        up.append(ring_send(up[-1], 1))
        down.append(ring_send(down[-1], -1))
    key_packed = deal.reshape(-1, 128)

    bucketed = bucket_rows(ranks, jnp.concatenate([q_half, hidden_in], axis=1))
    q_sent = bucketed[:, :width].reshape(RING, 2 * share, 2, HEAD_DIM)
    q_sent = q_sent.transpose(0, 2, 1, 3).reshape(shards, share, 2 * HEAD_DIM)
    h_sent = bucketed[:, width:].reshape(shards, share, width)
    moved = lax.all_to_all(jnp.concatenate([q_sent, h_sent], axis=2), TOK, 0, 0, tiled=True)
    sources = lax.dynamic_slice_in_dim(inverse, chip_row, 2 * rows) // rows
    q_places = sources * (2 * share) + within(sources)
    query = place_rows(q_places, moved[:, :, :width].reshape(2 * rows, HEAD_DIM))
    my_sources = lax.dynamic_slice_in_dim(inverse, first_row, rows) // rows
    residual = place_rows(
        my_sources * share + within(my_sources), moved[:, :, width:].reshape(rows, width)
    )
    q_start = start_of(chip_row + jnp.arange(2 * rows, dtype=jnp.int32))[None, :]

    place = [z, core]
    state = attend(
        query,
        q_start,
        key_packed,
        [(chunk, 0), (up[1], 0), (down[1], 0)],
        [z, (z - 1) % RING, (z + 1) % RING],
        place,
        None,
        False,
    )
    up[3], down[3], *state = lax.optimization_barrier((up[3], down[3], *state))
    far_low = ring_send(up[3][:rows], 1)
    far_high = ring_send(down[3][rows:], -1)
    state = attend(
        query,
        q_start,
        key_packed,
        [(up[2], 0), (down[2], 0), (up[3], 0), (down[3], 0)],
        [(z - 2) % RING, (z + 2) % RING, (z - 3) % RING, (z + 3) % RING],
        place,
        state,
        False,
    )
    state = attend(
        query,
        q_start,
        key_packed,
        [(far_low, 0), (far_high, rows)],
        [(z + 4) % RING] * 2,
        place,
        state,
        True,
    )
    attended = state[0]
    other = core_swap(attended[1])
    mine = attended[0]
    attended = jnp.where(
        core == 0,
        jnp.concatenate([mine, other], axis=1),
        jnp.concatenate([other, mine], axis=1),
    )

    slot_lines = slots.reshape(-1, 128)
    chosen = pick_rows(
        [(chunk, 0), (up[1], 0), (down[1], 0), (up[2], 0)],
        [z, (z - 1) % RING, (z + 1) % RING, (z - 2) % RING],
        slot_lines,
        core,
        chip_row,
        None,
        False,
    )
    pick_rest = functools.partial(
        pick_rows,
        [(down[2], 0), (up[3], 0), (down[3], 0), (far_low, 0), (far_high, rows)],
        [(z + 2) % RING, (z - 3) % RING, (z + 3) % RING, (z + 4) % RING, (z + 4) % RING],
        slot_lines,
        core,
        chip_row,
        last=True,
    )
    terms = output_terms(attended, w_out, core, x, y)
    mixed, chosen = scatter_features(terms, chosen, lambda before: pick_rest(acc=before))
    kept = jnp.where(core == 0, chosen[:rows], chosen[rows:])
    taken = core_swap(jnp.where(core == 0, chosen[rows:], chosen[:rows]))

    def by_head(at):
        own, swapped = kept[:, at : at + HEAD_DIM], taken[:, at : at + HEAD_DIM]
        low, high = jnp.where(core == 0, own, swapped), jnp.where(core == 0, swapped, own)
        return jnp.concatenate([low, high], axis=1)

    cache_keys, cache_values = by_head(0), by_head(HEAD_DIM)

    mixed_total = jnp.sum(spread(jnp.sum(mixed * mixed, axis=1)[None, :], REP, 16), axis=0)[0]
    normed = mixed * lax.rsqrt(mixed_total / full_width + EPSILON)[:, None] * post_gain[None, :]
    output = (residual.astype(jnp.float32) + normed).astype(jnp.bfloat16)
    return (output, cache_keys, cache_values)


def solution(mesh):
    grid = Mesh(mesh.devices.reshape(RING, 2, SIDE, SIDE), ("z", "core", "x", "y"))
    rows_by_features = P(TOK, REP)
    return jax.shard_map(
        body,
        mesh=grid,
        in_specs=(
            rows_by_features,
            P(None, REP),
            P(None, REP),
            P(None, REP),
            P(REP, None),
            P(REP),
            P(REP),
            P(REP),
            P(),
            P(),
            P(),
            P(),
            P(),
        ),
        out_specs=(rows_by_features,) * 3,
        check_vma=False,
    )
```

```python
import functools
import math

import jax
import jax.numpy as jnp
from jax import lax
from jax.experimental import pallas as pl
from jax.experimental.pallas import tpu as pltpu
from jax.sharding import Mesh
from jax.sharding import PartitionSpec as P

HEAD_DIM = 128
EPSILON = 1e-06
ROPE_BASE = 500000.0
SIDE = 4
RING = 8
TOK = ("z", "core")
REP = ("x", "y")
LOWEST = -1e30
FLOOR = -1e20
MATMUL_VMEM = 20 * 2**20
ATTEND_VMEM = 16 * 2**20


def plane_pairs(first, shift):
    pairs = []
    for core in range(2):
        for x in range(SIDE):
            for y in range(SIDE):
                along_x = (core == 0) == first
                to_x = (x + shift) % SIDE if along_x else x
                to_y = y if along_x else (y + shift) % SIDE
                pairs.append((core * 16 + x * 4 + y, core * 16 + to_x * 4 + to_y))
    return pairs


def plane_send(value, first, shift):
    return lax.ppermute(value, ("core", "x", "y"), plane_pairs(first, shift))


def ring_send(value, shift):
    return lax.ppermute(value, "z", [(i, (i + shift) % RING) for i in range(RING)])


def core_swap(value):
    return lax.ppermute(value, "core", [(0, 1), (1, 0)])


def spread(value, axes, size):
    copies = jnp.broadcast_to(value[None], (size, *value.shape))
    return lax.all_to_all(copies, axes, 0, 0, tiled=True)


def block_ids(steps, column, core, x, y):
    first = jnp.where(core == 0, x, y)
    second = (jnp.where(core == 0, y, x) + column) % SIDE
    mine = (first + jnp.array(steps, jnp.int32)) % SIDE
    return jnp.where(core == 0, mine * SIDE + second, second * SIDE + mine).astype(jnp.int32)


M_TILE = 512


def in_vmem(count):
    return [pl.BlockSpec(memory_space=pltpu.VMEM)] * count


def block_matmul(arrays, ids, weights, acc, finish=None, extras=(), outs=None):
    counts = [a.shape[0] for a in arrays]
    rows, depth = arrays[0].shape[1:]
    widths = [w.shape[1] for w in weights]
    total = sum(widths)
    blocks = sum(counts)
    n_arrays, n_weights, n_extras = len(arrays), len(weights), len(extras)
    has_acc = acc is not None
    if outs is None:
        outs = [jax.ShapeDtypeStruct((rows, total), jnp.float32)]

    def kernel(ids_ref, *refs):
        array_refs, refs = refs[:n_arrays], refs[n_arrays:]
        weight_refs, refs = refs[:n_weights], refs[n_weights:]
        if has_acc:
            acc_ref, refs = refs[0], refs[1:]
        extra_refs, out_refs = refs[:n_extras], refs[n_extras:]

        @pl.loop(0, rows // M_TILE)
        def _(tile):
            down = pl.ds(pl.multiple_of(tile * M_TILE, M_TILE), M_TILE)
            sums = []
            at = 0
            for w_ref, width in zip(weight_refs, widths):
                part = None
                block = 0
                for ref, count in zip(array_refs, counts):
                    for i in range(count):
                        first = pl.multiple_of(ids_ref[block] * depth, depth)
                        term = jnp.dot(
                            ref[i, down, :],
                            w_ref[pl.ds(first, depth), :],
                            preferred_element_type=jnp.float32,
                        )
                        part = term if part is None else part + term
                        block += 1
                if has_acc:
                    part = part + acc_ref[down, at : at + width]
                sums.append(part)
                at += width
            if finish is None:
                at = 0
                for part, width in zip(sums, widths):
                    out_refs[0][down, at : at + width] = part
                    at += width
            else:
                finish(sums, down, extra_refs, out_refs)

    operands = [*arrays, *weights, *([acc] if has_acc else []), *extras]
    return pl.pallas_call(
        kernel,
        grid_spec=pltpu.PrefetchScalarGridSpec(
            num_scalar_prefetch=1,
            grid=(1,),
            in_specs=in_vmem(len(operands)),
            out_specs=in_vmem(len(outs)),
        ),
        out_shape=outs,
        compiler_params=pltpu.CompilerParams(vmem_limit_bytes=MATMUL_VMEM),
        cost_estimate=pl.CostEstimate(
            flops=2 * rows * depth * total * blocks,
            bytes_accessed=blocks * depth * (rows + total) * 2 + rows * total * 8,
            transcendentals=0,
        ),
    )(ids, *operands)


def gather_features(block):
    left = plane_send(block, True, 1)
    right = plane_send(block, True, -1)
    far = plane_send(block, True, 2)
    pair = jnp.stack([block, left])
    pair_left = plane_send(pair, False, 1)
    pair_right = plane_send(pair, False, -1)
    other = jnp.stack([right, far])
    other_left = plane_send(other, False, 1)
    other_right = plane_send(other, False, -1)
    pair_far = plane_send(pair_left, False, 1)
    other_far = plane_send(other_right, False, -1)
    early = [
        (pair, [0, 3], 0),
        (other, [1, 2], 0),
        (pair_left, [0, 3], 3),
        (pair_right, [0, 3], 1),
        (other_left, [1, 2], 3),
        (other_right, [1, 2], 1),
    ]
    return early, [(pair_far, [0, 3], 2), (other_far, [1, 2], 2)]


def gathered_matmul(groups, weights, core, x, y, finish, extras, outs):
    ids = [
        jnp.concatenate([block_ids(steps, column, core, x, y) for _, steps, column in group])
        for group in groups
    ]
    early, late = ([a for a, _, _ in group] for group in groups)
    acc = block_matmul(early, ids[0], weights, None)[0]
    return block_matmul(late, ids[1], weights, acc, finish, extras, outs)


def finish_projection(parts, down, extras, outs):
    cos_ref, sin_ref, q_gain_ref, k_gain_ref = extras
    q_ref, k_ref, v_ref, sums_ref = outs
    query, key, value = parts
    q_sums = jnp.sum(query * query, axis=1, keepdims=True)
    k_sums = jnp.sum(key * key, axis=1, keepdims=True)
    lane = lax.broadcasted_iota(jnp.int32, (M_TILE, sums_ref.shape[1]), 1)
    sums_ref[down, :] = jnp.where(lane == 0, q_sums, k_sums)
    v_ref[down, :] = value.astype(jnp.bfloat16)
    cosine, sine = cos_ref[down, :], sin_ref[down, :]
    for part, gain_ref, ref in ((query, q_gain_ref, q_ref), (key, k_gain_ref, k_ref)):
        part = part * gain_ref[...]
        for head in range(2):
            at = slice(head * HEAD_DIM, (head + 1) * HEAD_DIM)
            one = part[:, at]
            ref[down, at] = one * cosine + pltpu.roll(one, HEAD_DIM // 2, 1) * sine


TERM_PLACE = ((0, 0), (0, 2), (3, 0), (1, 2), (1, 0), (2, 0), (2, 2), (4, 0))


def output_terms(attended, w_out, core, x, y):
    rows, width = attended.shape
    ids = jnp.concatenate([block_ids([0, 1, 2, 3], column, core, x, y) for column in range(4)])

    def kernel(ids_ref, a_ref, w_ref, *out_refs):
        for i in range(16):
            first = pl.multiple_of(ids_ref[i] * width, width)
            term = jnp.dot(
                a_ref[...], w_ref[:, pl.ds(first, width)], preferred_element_type=jnp.float32
            )
            out_refs[TERM_PLACE[i // 2][0]][TERM_PLACE[i // 2][1] + i % 2] = term.astype(jnp.bfloat16)

    return pl.pallas_call(
        kernel,
        grid_spec=pltpu.PrefetchScalarGridSpec(
            num_scalar_prefetch=1, grid=(1,), in_specs=in_vmem(2), out_specs=in_vmem(5)
        ),
        out_shape=[jax.ShapeDtypeStruct((n, rows, width), jnp.bfloat16) for n in (4, 4, 4, 2, 2)],
        compiler_params=pltpu.CompilerParams(vmem_limit_bytes=MATMUL_VMEM),
        cost_estimate=pl.CostEstimate(
            flops=32 * rows * width * width,
            bytes_accessed=34 * rows * width + 32 * width * width,
            transcendentals=0,
        ),
    )(ids, attended, w_out)


def added(*terms):
    total = terms[0].astype(jnp.float32)
    for term in terms[1:]:
        total = total + term.astype(jnp.float32)
    return total


def scatter_features(terms, first_gate, second_gate):
    near, up, down, plus, minus = terms
    from_up = plane_send(up, False, 1)
    from_down = plane_send(down, False, -1)
    last_up = plane_send(added(plus, from_up[:2]).astype(jnp.bfloat16), False, 1)
    last_down = plane_send(added(minus, from_down[:2]).astype(jnp.bfloat16), False, -1)
    last_up, last_down, first_gate = lax.optimization_barrier((last_up, last_down, first_gate))
    second = second_gate(first_gate)

    def part(i):
        if i < 2:
            return added(near[i], from_down[2 + i], last_up[i])
        return added(near[i], from_up[i], last_down[i - 2])

    sent = [
        plane_send(part(i).astype(jnp.bfloat16), True, shift)
        for i, shift in ((1, 1), (2, 2), (3, -1))
    ]
    *sent, second = lax.optimization_barrier((*sent, second))
    return part(0) + added(*sent), second


Q_TILE = 512
K_TILE = 512
A_TILE = 1024


def attend(query, q_start, key_packed, chunks, chips, place, state, last):
    rows = query.shape[0]
    n_chunks = len(chunks)
    has_state = state is not None
    lanes = key_packed.shape[1]
    per_chip = rows // lanes
    tiles = rows // Q_TILE

    def kernel(ids_ref, *refs):
        q_ref, start_ref, kp_ref, *refs = refs
        chunk_refs, refs = refs[:n_chunks], refs[n_chunks:]
        if has_state:
            top_in, total_in, sum_in, *refs = refs
        chip_at, core = ids_ref[n_chunks], ids_ref[n_chunks + 1]
        q_tile = q_ref[...]
        start = start_ref[...]
        packed = (
            chip_at * rows
            + pl.program_id(0) * Q_TILE
            + lax.broadcasted_iota(jnp.int32, (1, Q_TILE), 1)
        )
        if has_state:
            top, total, weighted = top_in[:1, :], total_in[:1, :], sum_in[...]
        else:
            top = jnp.full((1, Q_TILE), FLOOR, jnp.float32)
            total = jnp.zeros((1, Q_TILE), jnp.float32)
            weighted = jnp.zeros((HEAD_DIM, Q_TILE), jnp.float32)
        for i, (ref, (array, first)) in enumerate(zip(chunk_refs, chunks)):
            k_tile = min(A_TILE, array.shape[0])
            for at in range(0, array.shape[0], k_tile):
                keys = ref[at : at + k_tile, :HEAD_DIM]
                values = ref[at : at + k_tile, HEAD_DIM:]
                columns = []
                for k in range(k_tile // lanes):
                    group = (first + at) // lanes + k
                    row = lax.rem(group + core * (per_chip // 2), per_chip)
                    line = kp_ref[pl.ds(ids_ref[i] * per_chip + row, 1), :]
                    columns.append(jnp.broadcast_to(line, (lanes, lanes)).T)
                kp = jnp.concatenate(columns, axis=0)
                kp = jnp.concatenate([kp] * (Q_TILE // lanes), axis=1)
                scores = lax.dot_general(
                    keys, q_tile, (((1,), (1,)), ((), ())), preferred_element_type=jnp.float32
                )
                allowed = (kp <= packed) & (kp >= start)
                scores = jnp.where(allowed, scores, LOWEST)
                new_top = jnp.maximum(top, jnp.max(scores, axis=0, keepdims=True))
                weights = jnp.exp2(scores - new_top)
                factor = jnp.exp2(top - new_top)
                total = total * factor + jnp.sum(weights, axis=0, keepdims=True)
                weighted = weighted * factor + lax.dot_general(
                    values,
                    weights.astype(jnp.bfloat16),
                    (((0,), (0,)), ((), ())),
                    preferred_element_type=jnp.float32,
                )
                top = new_top
        if last:
            refs[0][0] = (weighted / total).T.astype(jnp.bfloat16)
        else:
            top_out, total_out, sum_out = refs
            top_out[...] = jnp.broadcast_to(top, top_out.shape)
            total_out[...] = jnp.broadcast_to(total, total_out.shape)
            sum_out[...] = weighted

    def across(height):
        return pl.BlockSpec((height, Q_TILE), lambda i, ids_ref: (0, i))

    in_specs = [pl.BlockSpec((Q_TILE, HEAD_DIM), lambda i, ids_ref: (i, 0)), across(1)]
    in_specs += in_vmem(1 + n_chunks)
    operands = [query, q_start, key_packed, *[a for a, _ in chunks]]
    if has_state:
        in_specs += [across(8), across(8), across(HEAD_DIM)]
        operands += list(state)
    if last:
        out_shape = [jax.ShapeDtypeStruct((tiles, Q_TILE, HEAD_DIM), jnp.bfloat16)]
        out_specs = [
            pl.BlockSpec(
                (1, Q_TILE, HEAD_DIM),
                lambda i, ids_ref: (lax.rem(i + ids_ref[n_chunks + 1], tiles), 0, 0),
            )
        ]
    else:
        out_shape = [jax.ShapeDtypeStruct((8, rows), jnp.float32)] * 2
        out_shape.append(jax.ShapeDtypeStruct((HEAD_DIM, rows), jnp.float32))
        out_specs = [across(8), across(8), across(HEAD_DIM)]
    keys_seen = sum(a.shape[0] for a, _ in chunks)
    ids = jnp.concatenate([jnp.stack(chips), jnp.stack(place)]).astype(jnp.int32)
    return pl.pallas_call(
        kernel,
        grid_spec=pltpu.PrefetchScalarGridSpec(
            num_scalar_prefetch=1,
            grid=(tiles,),
            in_specs=in_specs,
            out_specs=out_specs,
        ),
        out_shape=out_shape,
        compiler_params=pltpu.CompilerParams(vmem_limit_bytes=ATTEND_VMEM),
        cost_estimate=pl.CostEstimate(
            flops=4 * rows * keys_seen * HEAD_DIM,
            bytes_accessed=rows * HEAD_DIM * 10 + keys_seen * 1024,
            transcendentals=0,
        ),
    )(ids, *operands)


C_TILE = 256


def pick_rows(chunks, chips, slot_lines, core, row_base, acc, last):
    n_chunks = len(chunks)
    lanes = slot_lines.shape[1]
    rows = 2 * K_TILE
    per_chip = rows // lanes
    width = chunks[0][0].shape[1]
    has_acc = acc is not None

    def kernel(ids_ref, lines_ref, *refs):
        chunk_refs, refs = refs[:n_chunks], refs[n_chunks:]
        tile = pl.program_id(0)
        mine = (
            ids_ref[n_chunks + 1] + tile * C_TILE + lax.broadcasted_iota(jnp.int32, (C_TILE, 1), 0)
        )
        total = refs[0][...] if has_acc else jnp.zeros((C_TILE, width), jnp.float32)
        for i, (ref, (array, first)) in enumerate(zip(chunk_refs, chunks)):
            for at in range(0, array.shape[0], K_TILE):
                chosen = []
                for k in range(K_TILE // lanes):
                    group = (first + at) // lanes + k
                    row = lax.rem(group + ids_ref[n_chunks] * (per_chip // 2), per_chip)
                    line = lines_ref[pl.ds(ids_ref[i] * per_chip + row, 1), :]
                    chosen.append(jnp.where(line == mine, 1.0, 0.0).astype(jnp.bfloat16))
                total = total + jnp.dot(
                    jnp.concatenate(chosen, axis=1),
                    ref[at : at + K_TILE, :],
                    preferred_element_type=jnp.float32,
                )
        refs[-1][...] = total.astype(refs[-1].dtype)

    def tile_spec():
        return pl.BlockSpec((C_TILE, width), lambda i, ids_ref: (i, 0))

    operands = [slot_lines, *[a for a, _ in chunks], *([acc] if has_acc else [])]
    ids = jnp.stack([*chips, core, row_base]).astype(jnp.int32)
    keys_seen = sum(a.shape[0] for a, _ in chunks)
    return pl.pallas_call(
        kernel,
        grid_spec=pltpu.PrefetchScalarGridSpec(
            num_scalar_prefetch=1,
            grid=(rows // C_TILE,),
            in_specs=in_vmem(1 + n_chunks) + ([tile_spec()] if has_acc else []),
            out_specs=[tile_spec()],
        ),
        out_shape=[jax.ShapeDtypeStruct((rows, width), jnp.bfloat16 if last else jnp.float32)],
        compiler_params=pltpu.CompilerParams(vmem_limit_bytes=ATTEND_VMEM),
        cost_estimate=pl.CostEstimate(
            flops=2 * rows * keys_seen * width,
            bytes_accessed=rows * width * 6 + keys_seen * width * 2,
            transcendentals=0,
        ),
    )(ids, *operands)[0]


def ranks_of(values):
    return jnp.sum((values[None, :] < values[:, None]).astype(jnp.int32), axis=1)


def within(sources):
    index = jnp.arange(sources.shape[0], dtype=jnp.int32)
    same = (sources[None, :] == sources[:, None]) & (index[None, :] < index[:, None])
    return jnp.sum(same.astype(jnp.int32), axis=1)


def place_rows(positions, rows):
    index = jnp.arange(rows.shape[0], dtype=jnp.int32)
    chosen = (positions[:, None] == index[None, :]).astype(jnp.bfloat16)
    return jnp.dot(chosen, rows, preferred_element_type=jnp.float32).astype(jnp.bfloat16)


def bucket_rows(ranks, rows):
    index = jnp.arange(rows.shape[0], dtype=jnp.int32)
    chosen = (ranks[None, :] == index[:, None]).astype(jnp.bfloat16)
    return jnp.dot(chosen, rows, preferred_element_type=jnp.float32).astype(jnp.bfloat16)


def body(
    hidden_in,
    w_query,
    w_key,
    w_value,
    w_out,
    q_gain,
    k_gain,
    post_gain,
    prompt_lengths,
    segment_ids,
    deal,
    inverse,
    slots,
):
    rows, width = hidden_in.shape
    full_width = w_query.shape[0]
    shards = 16
    share = rows // shards
    x, y = lax.axis_index("x"), lax.axis_index("y")
    z, core = lax.axis_index("z"), lax.axis_index("core")
    first_row = (z * 2 + core) * rows
    chip_row = z * 2 * rows

    prompt_ids = jnp.arange(prompt_lengths.shape[0], dtype=jnp.int32)
    prompt_starts = jnp.sum(
        jnp.where(prompt_ids[None, :] < prompt_ids[:, None], prompt_lengths[None, :], 0), axis=1
    )

    def start_of(packed):
        return jnp.max(
            jnp.where(prompt_starts[None, :] <= packed[:, None], prompt_starts[None, :], 0), axis=1
        )

    my_packed = lax.dynamic_slice_in_dim(deal, first_row, rows)
    positions = (my_packed - start_of(my_packed)).astype(jnp.float32)
    half = HEAD_DIM // 2
    frequency = ROPE_BASE ** (-jnp.arange(half, dtype=jnp.float32) * 2.0 / HEAD_DIM)
    angles = positions[:, None] * frequency[None, :]
    cosine, sine = jnp.cos(angles), jnp.sin(angles)
    cosine = jnp.concatenate([cosine, cosine], axis=1)
    sine = jnp.concatenate([-sine, sine], axis=1)

    ranks = ranks_of(my_packed)
    groups = gather_features(hidden_in)
    float_rows = jax.ShapeDtypeStruct((rows, width), jnp.float32)
    half_rows = jax.ShapeDtypeStruct((rows, width), jnp.bfloat16)
    lane_rows = jax.ShapeDtypeStruct((rows, 128), jnp.float32)
    q_rot, k_rot, value, sums = gathered_matmul(
        groups,
        [w_query, w_key, w_value],
        core,
        x,
        y,
        finish_projection,
        [cosine, sine, q_gain[None, :], k_gain[None, :]],
        [float_rows, float_rows, half_rows, lane_rows],
    )

    all_sums = jnp.sum(spread(sums[:, :2].T, REP, 16), axis=0)
    scales = lax.rsqrt(all_sums / full_width + EPSILON)
    to_scores = HEAD_DIM**-0.5 * math.log2(math.e)
    q_half = (q_rot * (scales[0] * to_scores)[:, None]).astype(jnp.bfloat16)
    k_half = (k_rot * scales[1][:, None]).astype(jnp.bfloat16)

    def own_head(both):
        return jnp.where(core == 0, both[:, :HEAD_DIM], both[:, HEAD_DIM:])

    def other_head(both):
        return jnp.where(core == 0, both[:, HEAD_DIM:], both[:, :HEAD_DIM])

    kept = jnp.concatenate([own_head(k_half), own_head(value)], axis=1)
    given = jnp.concatenate([other_head(k_half), other_head(value)], axis=1)
    chunk = jnp.concatenate([kept, core_swap(given)])

    up, down = [chunk], [chunk]
    for _ in range(3):
        up.append(ring_send(up[-1], 1))
        down.append(ring_send(down[-1], -1))
    key_packed = deal.reshape(-1, 128)

    bucketed = bucket_rows(ranks, jnp.concatenate([q_half, hidden_in], axis=1))
    q_sent = bucketed[:, :width].reshape(RING, 2 * share, 2, HEAD_DIM)
    q_sent = q_sent.transpose(0, 2, 1, 3).reshape(shards, share, 2 * HEAD_DIM)
    h_sent = bucketed[:, width:].reshape(shards, share, width)
    moved = lax.all_to_all(jnp.concatenate([q_sent, h_sent], axis=2), TOK, 0, 0, tiled=True)
    sources = lax.dynamic_slice_in_dim(inverse, chip_row, 2 * rows) // rows
    q_places = sources * (2 * share) + within(sources)
    query = place_rows(q_places, moved[:, :, :width].reshape(2 * rows, HEAD_DIM))
    my_sources = lax.dynamic_slice_in_dim(inverse, first_row, rows) // rows
    residual = place_rows(
        my_sources * share + within(my_sources), moved[:, :, width:].reshape(rows, width)
    )
    q_start = start_of(chip_row + jnp.arange(2 * rows, dtype=jnp.int32))[None, :]

    place = [z, core]
    state = attend(
        query,
        q_start,
        key_packed,
        [(chunk, 0), (up[1], 0), (down[1], 0)],
        [z, (z - 1) % RING, (z + 1) % RING],
        place,
        None,
        False,
    )
    up[3], down[3], *state = lax.optimization_barrier((up[3], down[3], *state))
    far_low = ring_send(up[3][:rows], 1)
    far_high = ring_send(down[3][rows:], -1)
    state = attend(
        query,
        q_start,
        key_packed,
        [(up[2], 0), (down[2], 0), (up[3], 0), (down[3], 0)],
        [(z - 2) % RING, (z + 2) % RING, (z - 3) % RING, (z + 3) % RING],
        place,
        state,
        False,
    )
    state = attend(
        query,
        q_start,
        key_packed,
        [(far_low, 0), (far_high, rows)],
        [(z + 4) % RING] * 2,
        place,
        state,
        True,
    )
    attended = state[0]
    other = core_swap(attended[1])
    mine = attended[0]
    attended = jnp.where(
        core == 0,
        jnp.concatenate([mine, other], axis=1),
        jnp.concatenate([other, mine], axis=1),
    )

    slot_lines = slots.reshape(-1, 128)
    chosen = pick_rows(
        [(chunk, 0), (up[1], 0), (down[1], 0), (up[2], 0)],
        [z, (z - 1) % RING, (z + 1) % RING, (z - 2) % RING],
        slot_lines,
        core,
        chip_row,
        None,
        False,
    )
    pick_rest = functools.partial(
        pick_rows,
        [(down[2], 0), (up[3], 0), (down[3], 0), (far_low, 0), (far_high, rows)],
        [(z + 2) % RING, (z - 3) % RING, (z + 3) % RING, (z + 4) % RING, (z + 4) % RING],
        slot_lines,
        core,
        chip_row,
        last=True,
    )
    terms = output_terms(attended, w_out, core, x, y)
    mixed, chosen = scatter_features(terms, chosen, lambda before: pick_rest(acc=before))
    kept = jnp.where(core == 0, chosen[:rows], chosen[rows:])
    taken = core_swap(jnp.where(core == 0, chosen[rows:], chosen[:rows]))
    mixed, taken = lax.optimization_barrier((mixed, taken))

    def by_head(at):
        own, swapped = kept[:, at : at + HEAD_DIM], taken[:, at : at + HEAD_DIM]
        low, high = jnp.where(core == 0, own, swapped), jnp.where(core == 0, swapped, own)
        return jnp.concatenate([low, high], axis=1)

    cache_keys, cache_values = by_head(0), by_head(HEAD_DIM)

    mixed_total = jnp.sum(spread(jnp.sum(mixed * mixed, axis=1)[None, :], REP, 16), axis=0)[0]
    normed = mixed * lax.rsqrt(mixed_total / full_width + EPSILON)[:, None] * post_gain[None, :]
    output = (residual.astype(jnp.float32) + normed).astype(jnp.bfloat16)
    return (output, cache_keys, cache_values)


def solution(mesh):
    grid = Mesh(mesh.devices.reshape(RING, 2, SIDE, SIDE), ("z", "core", "x", "y"))
    rows_by_features = P(TOK, REP)
    return jax.shard_map(
        body,
        mesh=grid,
        in_specs=(
            rows_by_features,
            P(None, REP),
            P(None, REP),
            P(None, REP),
            P(REP, None),
            P(REP),
            P(REP),
            P(REP),
            P(),
            P(),
            P(),
            P(),
            P(),
        ),
        out_specs=(rows_by_features,) * 3,
        check_vma=False,
    )
```
